32 devices in a mesh: spec: 4 (over y, x), geo: 8 (over z, core).
Axes of the slice: x: 2, y: 2, z: 4, core: 2. Of those that a mesh axis runs over, the one named last changes fastest.
Arguments:
- spectrum: bfloat16 [1296, 128, 128], P('spec', 'geo'), may hold values from 0.01 to 11, as said below
- sea_map: int32 [128, 128], P('geo'), may hold values 0 or 1
- depth_factor: float32 [128, 128], P('geo'), may hold values from 0.25 to 1
- wind_speed: bfloat16 [128, 128], P('geo'), may hold values from 0.19921875 to 2
- wind_dir: bfloat16 [128, 128], P('geo'), may hold values from -3.140625 to 3.140625
- ice_mask: int32 [128, 128], P('geo'), may hold values from 0 to 1, as said below
- owner_map: int32 [128, 128], P('geo'), may hold values from 0 to 7, as said below
- pair_kernel: bfloat16 [1296, 1296], replicated, may hold values from -1 to 2
- transfer_kernel: bfloat16 [8, 1296, 1296], P('geo'), may hold values from -1 to 2
Outputs:
- updated: bfloat16 [1296, 128, 128], P('spec', 'geo')
The draws below stay inside these ranges and needn't reach their ends.
Inputs may be any that keep to these rules, and one draw needn't show every extreme that they name: `owner_map`: in each aligned block of 512 cells of the grid in row-major order, no owner is named by more than 128 cells, and one owner, the same in every block, is named by exactly 128 cells of each block. `ice_mask`: 1 marks ice. Cells of the owner that is named by 128 cells of every block are free of ice. `spectrum`: Positive.
All inputs are finite; a program needn't handle non-finite values. No bound on the sum of `sea_map` on one device may be relied on, other than what follows from the above.
Results may differ from the reference program's by a relative error of at most 0.0059.
Values may be sent and summed in bfloat16 or wider, within the bound.
No kernel may reach another device: no remote copies, remote signals or barrier semaphores. Data moves between devices by JAX's collectives and lax.ppermute only.
A program may use at most 64 MiB of HBM per device.

```python
import math
import jax
import jax.numpy as jnp
from jax import lax

NDIR = 36
NFREQ = 36
COMP = 1296
CY = 128
NX = 128
ROWS_DEV = 512
CAP = 128
TILES = 8


def routing_tables(key):
    base = jax.random.fold_in(key, 7001)
    key_hot, key_blocks, key_ice = jax.random.split(base, 3)
    block_count = NX * CY // ROWS_DEV
    hottest = jax.random.randint(key_hot, (), 0, TILES).astype(jnp.int32)
    spread_rows = ROWS_DEV - CAP
    others = TILES - 1
    levels = jnp.arange(others + 1, dtype=jnp.int32)
    bounds = spread_rows * (17 * levels * others - 7 * levels * levels) // (10 * others * others)
    position = jnp.arange(ROWS_DEV, dtype=jnp.int32)
    shifted = position - CAP
    tier = jnp.sum((bounds[None, 1:] <= shifted[:, None]).astype(jnp.int32), axis=1)
    tier = jnp.minimum(tier, others - 1)

    def one_block(block_key):
        key_order, key_place = jax.random.split(block_key)
        order = jax.random.permutation(key_order, others).astype(jnp.int32)
        chosen = (hottest + 1 + order[tier]) % TILES
        ranked = jnp.where(position < CAP, hottest, chosen).astype(jnp.int32)
        placed = jax.random.permutation(key_place, ROWS_DEV)
        return jnp.zeros((ROWS_DEV,), jnp.int32).at[placed].set(ranked)
    owners = jax.vmap(one_block)(jax.random.split(key_blocks, block_count)).reshape(NX, CY)
    frozen = jax.random.randint(key_ice, (NX, CY), 0, 8) == 0
    ice = jnp.where(frozen & (owners != hottest), 1, 0).astype(jnp.int32)
    return (owners.astype(jnp.int32), ice)


def draw_owner_map(key, part):
    owners, ice = routing_tables(key)
    return owners


def draw_ice_mask(key, part):
    owners, ice = routing_tables(key)
    return ice


def draw_spectrum(key, part):
    base = jax.random.fold_in(key, 7101)
    key_cell, key_profile, key_rough = jax.random.split(base, 3)
    cell_scale = jnp.exp(jax.random.uniform(key_cell, (1, NX, CY), jnp.float32, math.log(0.2), math.log(2.0)))
    profile = jnp.exp(jax.random.uniform(key_profile, (COMP, 1, 1), jnp.float32, math.log(0.3), math.log(3.0)))
    rough = jax.random.uniform(key_rough, (COMP, NX, CY), jnp.float32, 0.5, 1.5)
    return (cell_scale * profile * rough).astype(jnp.bfloat16)


def kernel_matrix(key, leading, off_scale):
    key_diag, key_off = jax.random.split(key)
    diagonal = jax.random.uniform(key_diag, leading + (COMP,), jnp.float32, 0.5, 1.5)
    off_part = jax.random.truncated_normal(key_off, -3.0, 3.0, leading + (COMP, COMP), jnp.float32)
    index = jnp.arange(COMP, dtype=jnp.int32)
    identity = (index[:, None] == index[None, :]).astype(jnp.float32)
    return identity * diagonal[..., :, None] + off_part * (off_scale / math.sqrt(COMP))


def draw_pair_kernel(key, part):
    return kernel_matrix(jax.random.fold_in(key, 7201), (), 0.8).astype(jnp.bfloat16)


def draw_transfer_kernel(key, part):
    return kernel_matrix(jax.random.fold_in(key, 7301), (TILES,), 0.6).astype(jnp.bfloat16)


def with_ends(values, stream_key, smallest, largest):
    longest = values.shape.index(max(values.shape))
    spots = []
    for shift in (0, 1):
        where = [jax.random.randint(jax.random.fold_in(stream_key, axis), (), 0, length) for axis, length in enumerate(values.shape)]
        where[longest] = (where[longest] + shift) % values.shape[longest]
        spots.append(tuple(where))
    return values.at[spots[0]].set(smallest).at[spots[1]].set(largest)


def block_scale(rng, dims, pieces, low, top_value):
    loudness = 1.0
    for dim, shards_of in pieces:
        heights = jax.random.uniform(jax.random.fold_in(jax.random.fold_in(rng, 6), dim), (shards_of,), jnp.float32, low / len(pieces), top_value / len(pieces))
        loudness = loudness * jnp.repeat(jnp.exp(heights), dims[dim] // shards_of).reshape((-1,) + (1,) * (len(dims) - 1 - dim))
    return loudness


def setup_inputs(seed: int = 0) -> dict:
    key_list = jax.random.split(jax.random.key(seed), 10)
    return {
        "spectrum": draw_spectrum(jax.random.fold_in(key_list[9], 71), 0),
        "sea_map": with_ends((jax.random.randint(key_list[1], (NX, CY), 0, 8) < 7).astype(jnp.int32), jax.random.fold_in(key_list[1], 1), 0, 1),
        "depth_factor": jnp.clip(jnp.exp(math.log(1.0) - 1.3862944 * jax.random.uniform(key_list[2], (NX, CY), jnp.float32) ** block_scale(key_list[2], (NX, CY), ((0, 8),), -0.2, 0.2)), 0.25, 1.0),
        "wind_speed": jnp.clip(jnp.exp(math.log(2.0) - 2.306499 * jax.random.uniform(key_list[3], (NX, CY), jnp.float32) ** block_scale(key_list[3], (NX, CY), ((0, 8),), -0.2, 0.2)), 0.19921875, 2.0).astype(jnp.bfloat16),
        "wind_dir": jnp.clip(jax.random.uniform(key_list[4], (NX, CY), jnp.float32, -3.140625, 3.140625), -3.140625, 3.140625).astype(jnp.bfloat16),
        "ice_mask": draw_ice_mask(jax.random.fold_in(key_list[9], 71), 0),
        "owner_map": draw_owner_map(jax.random.fold_in(key_list[9], 71), 0),
        "pair_kernel": draw_pair_kernel(jax.random.fold_in(key_list[9], 71), 0),
        "transfer_kernel": draw_transfer_kernel(jax.random.fold_in(key_list[9], 71), 0),
    }


def finish(row_data, transfer, wind_rows, wind_angle):
    energy = row_data.astype(jnp.float32)
    total = jnp.mean(energy, axis=0)
    ratio = total / (1.0 + total)
    component = jnp.arange(row_data.shape[0], dtype=jnp.int32)
    heading = 2.0 * math.pi * ((component % NDIR).astype(jnp.float32) + 0.5) / NDIR
    forcing = 0.3 * wind_rows.astype(jnp.float32)[None, :] * jnp.maximum(jnp.cos(heading[:, None] - wind_angle.astype(jnp.float32)[None, :]), 0.0)
    result = energy * (1.0 + forcing - 0.5 * ratio[None, :]) + 0.2 * transfer.astype(jnp.float32) / (1.0 + total)[None, :]
    return result.astype(jnp.bfloat16)


def propagate(spectrum, sea_map, depth_factor):
    sea_weight = sea_map.astype(jnp.float32)
    depth_cell = depth_factor.astype(jnp.float32)
    heading = 2.0 * math.pi * (jnp.arange(NDIR, dtype=jnp.int32).astype(jnp.float32) + 0.5) / NDIR
    cosine = jnp.cos(heading)[:, None, None]
    sine = jnp.sin(heading)[:, None, None]
    bands = spectrum.reshape(NFREQ, NDIR, NX, CY)
    frequency = jnp.arange(NFREQ, dtype=jnp.int32).astype(jnp.float32)

    def advect_band(item):
        band_freq, band = item
        centre = band.astype(jnp.float32) * sea_weight
        gain = jnp.float32(1.1) ** (-0.5 * band_freq)
        step_x = 0.7 * gain * jnp.abs(cosine) * depth_cell
        step_y = 0.7 * gain * jnp.abs(sine) * depth_cell
        zeros_x = jnp.zeros((NDIR, 1, CY), jnp.float32)
        zeros_y = jnp.zeros((NDIR, NX, 1), jnp.float32)
        west_side = jnp.concatenate([zeros_x, centre[:, :-1]], axis=1)
        east_side = jnp.concatenate([centre[:, 1:], zeros_x], axis=1)
        south_side = jnp.concatenate([zeros_y, centre[:, :, :-1]], axis=2)
        north_side = jnp.concatenate([centre[:, :, 1:], zeros_y], axis=2)
        upwind_x = jnp.where(cosine > 0, west_side, east_side)
        upwind_y = jnp.where(sine > 0, south_side, north_side)
        advected = centre - step_x * (centre - upwind_x) - step_y * (centre - upwind_y)
        return (advected * sea_weight).astype(jnp.bfloat16)

    return lax.map(advect_band, (frequency, bands)).reshape(COMP, NX * CY)


def slot_numbers(owners):
    onehot = (owners[:, None] == jnp.arange(TILES, dtype=jnp.int32)[None, :]).astype(jnp.int32)
    before = jnp.cumsum(onehot, axis=0) - onehot
    position = jnp.sum(before * onehot, axis=1)
    return (owners * CAP + position).astype(jnp.int32)


def reference(spectrum, sea_map, depth_factor, wind_speed, wind_dir, ice_mask, owner_map, pair_kernel, transfer_kernel):
    block_count = NX * CY // ROWS_DEV
    propagated = propagate(spectrum, sea_map, depth_factor)
    blocks = propagated.reshape(COMP, block_count, ROWS_DEV).transpose(1, 0, 2)
    owner_blocks = owner_map.reshape(block_count, ROWS_DEV)
    slot_blocks = lax.map(slot_numbers, owner_blocks)

    def pair_block(item):
        row_data, slot_index = item
        coupled = jnp.dot(pair_kernel, row_data, preferred_element_type=jnp.float32)
        paired = (row_data.astype(jnp.float32) * coupled).astype(jnp.bfloat16)
        return jnp.zeros((COMP, TILES * CAP), jnp.bfloat16).at[:, slot_index].set(paired)

    packed = lax.map(pair_block, (blocks, slot_blocks))
    per_owner = packed.reshape(block_count, COMP, TILES, CAP).transpose(2, 1, 0, 3).reshape(TILES, COMP, block_count * CAP)

    def apply_kernel(item):
        own_kernel, columns = item
        return jnp.dot(own_kernel, columns, preferred_element_type=jnp.float32).astype(jnp.bfloat16)

    transfer = lax.map(apply_kernel, (transfer_kernel, per_owner))
    returned = transfer.reshape(TILES, COMP, block_count, CAP).transpose(2, 1, 0, 3).reshape(block_count, COMP, TILES * CAP)

    def finish_block(item):
        row_data, slot_index, back_block, frozen, wind_rows, wind_angle = item
        terms = back_block[:, slot_index]
        sourced = finish(row_data, terms, wind_rows, wind_angle)
        return jnp.where(frozen[None, :] == 1, row_data, sourced)

    finished = lax.map(finish_block, (blocks, slot_blocks, returned, ice_mask.reshape(block_count, ROWS_DEV), wind_speed.reshape(block_count, ROWS_DEV), wind_dir.reshape(block_count, ROWS_DEV)))
    return finished.transpose(1, 0, 2).reshape(COMP, NX, CY)
```

```python
import functools
import math

import jax
import jax.numpy as jnp
from jax import lax
from jax.experimental import pallas as pl
from jax.experimental.pallas import tpu as pltpu
from jax.sharding import Mesh
from jax.sharding import PartitionSpec as P

NDIR = 36
PLANES = 4
SUB = 16
VMEM = pl.BlockSpec(memory_space=pltpu.VMEM)
SMEM = pl.BlockSpec(memory_space=pltpu.SMEM)
BF16 = jnp.bfloat16
F32 = jnp.float32


def params(mib=14):
    return pltpu.CompilerParams(vmem_limit_bytes=mib * 2**20)


def propagate_kernel(wanted, x_ref, west_ref, east_ref, sea_ref, depth_ref, coef_ref, out_ref):
    rows, comps, width = x_ref.shape

    def tile(at, height):
        lane = lax.broadcasted_iota(jnp.int32, (height, width), 1)
        coef = coef_ref[at, :]
        gain_x, gain_y, pos_x, pos_y = (
            jnp.broadcast_to(coef[:, i : i + 1], (height, width)) for i in range(4)
        )
        from_west, from_south = pos_x > 0, pos_y > 0
        first, last = lane == 0, lane == width - 1
        known = {}

        def masked(row):
            if row not in known:
                if row < 0:
                    known[row] = west_ref[at, :].astype(F32)
                elif row == rows:
                    known[row] = east_ref[at, :].astype(F32)
                else:
                    known[row] = x_ref[row, at, :].astype(F32) * sea_ref[row : row + 1, :]
            return known[row]

        for k, row in enumerate(wanted):
            west, centre, east = masked(row - 1), masked(row), masked(row + 1)
            upwind_x = jnp.where(from_west, west, east)
            south = jnp.where(first, 0.0, pltpu.roll(centre, 1, 1))
            north = jnp.where(last, 0.0, pltpu.roll(centre, width - 1, 1))
            upwind_y = jnp.where(from_south, south, north)
            depth = depth_ref[row : row + 1, :]
            moved = (
                centre
                - gain_x * depth * (centre - upwind_x)
                - gain_y * depth * (centre - upwind_y)
            )
            out_ref[at, k * width : (k + 1) * width] = (
                moved * sea_ref[row : row + 1, :]
            ).astype(BF16)

    def body(step, carry):
        tile(pl.ds(pl.multiple_of(step * SUB, SUB), SUB), SUB)
        return carry

    whole = comps // SUB
    lax.fori_loop(0, whole, body, 0)
    if comps % SUB:
        spare = out_ref.shape[0] - whole * SUB
        out_ref[whole * SUB :, :] = jnp.zeros((spare, out_ref.shape[1]), BF16)
        tile(slice(whole * SUB, comps), comps - whole * SUB)


def propagate(wanted, x, west, east, sea, depth, coef):
    comps, width = x.shape[1:]
    padded = -(-comps // SUB) * SUB
    cells = len(wanted) * width
    return pl.pallas_call(
        functools.partial(propagate_kernel, wanted),
        out_shape=jax.ShapeDtypeStruct((padded, cells), BF16),
        in_specs=[VMEM] * 6,
        out_specs=VMEM,
        compiler_params=params(),
        cost_estimate=pl.CostEstimate(
            flops=2 * comps * cells, bytes_accessed=comps * cells, transcendentals=0
        ),
    )(x, west, east, sea, depth, coef)


def pair_kernel_body(tile, comps, here_ref, *refs):
    *parts, pair_ref, out_ref, mean_ref, whole = refs
    step = pl.program_id(0)

    @pl.when(step == 0)
    def _():
        for here in range(4):

            @pl.when(here_ref[0] == here)
            def _(here=here):
                for flip, part in enumerate(parts[:3]):
                    at = (here ^ flip) * comps
                    whole[at : at + comps, :] = part[:comps, :]
                at, column = (here ^ 3) * comps, 0
                for part in parts[3:]:
                    width = part.shape[1]
                    whole[at : at + comps, column : column + width] = part[:comps, :]
                    column += width

        total = jnp.sum(whole[...].astype(F32), axis=0, keepdims=True)
        mean_ref[...] = total / whole.shape[0]

    coupled = jnp.dot(pair_ref[...], whole[...], preferred_element_type=F32)
    own = whole[pl.ds(pl.multiple_of(step * tile, SUB), tile), :]
    out_ref[...] = (own.astype(F32) * coupled).astype(BF16)


def pair_up(here, parts, pair, tile=432):
    comps, cells = pair.shape[0], parts[0].shape[1]
    specs = [pl.BlockSpec(part.shape, lambda i: (0, 0)) for part in parts]
    return pl.pallas_call(
        functools.partial(pair_kernel_body, tile, comps // 4),
        grid=(comps // tile,),
        out_shape=[jax.ShapeDtypeStruct((comps, cells), BF16), jax.ShapeDtypeStruct((1, cells), F32)],
        in_specs=[SMEM] + specs + [pl.BlockSpec((tile, comps), lambda i: (i, 0))],
        out_specs=[
            pl.BlockSpec((tile, cells), lambda i: (i, 0)),
            pl.BlockSpec((1, cells), lambda i: (0, 0)),
        ],
        scratch_shapes=[pltpu.VMEM((comps, cells), BF16)],
        compiler_params=params(),
        cost_estimate=pl.CostEstimate(
            flops=comps * comps * cells // 4, bytes_accessed=comps * comps // 4, transcendentals=0
        ),
    )(here, *parts, pair)


def apply_owned(ids_ref, owner, paired, kernels, held):
    for number, kernel in enumerate(kernels):
        term = jnp.dot(kernel[...], paired, preferred_element_type=F32)
        held = jnp.where(owner == ids_ref[number], term, held)
    return held


def listed(found):
    return jnp.stack([owner for _, owner in found]).astype(jnp.int32), [k for k, _ in found]


def split(refs, *sizes):
    out, at = [], 0
    for size in sizes:
        out.append(refs[at : at + size])
        at += size
    return out


def transfer_body(count, chunks, first, ids_ref, *refs):
    kernels, owners, paired, held, outs = split(
        refs, count, chunks, chunks, 0 if first else chunks, chunks
    )
    for chunk, out_ref in enumerate(outs):
        value = jnp.zeros(out_ref.shape, F32) if first else held[chunk][...].astype(F32)
        value = apply_owned(ids_ref, owners[chunk][...], paired[chunk][...], kernels, value)
        out_ref[...] = value.astype(BF16)


def transfer_cost(kernels, paired):
    flops = len(kernels) * kernels[0].size * sum(p.shape[1] for p in paired)
    moved = 2 * (len(kernels) * kernels[0].size + sum(p.size for p in paired))
    return pl.CostEstimate(flops=flops // 4, bytes_accessed=moved // 8, transcendentals=0)


def transfer_part(found, owners, paired, held):
    ids, kernels = listed(found)
    operands = [*kernels, *owners, *paired, *(held or [])]
    shapes = [jax.ShapeDtypeStruct((kernels[0].shape[0], p.shape[1]), BF16) for p in paired]
    return pl.pallas_call(
        functools.partial(transfer_body, len(kernels), len(paired), held is None),
        out_shape=shapes,
        in_specs=[SMEM] + [VMEM] * len(operands),
        out_specs=[VMEM] * len(shapes),
        compiler_params=params(),
        cost_estimate=transfer_cost(kernels, paired),
    )(ids, *operands)


def transfer(found, owners, paired, held, most=6):
    for at in range(0, len(found), most):
        held = transfer_part(found[at : at + most], owners, paired, held)
    return list(held)


def finish_body(count, groups, ids_ref, angle_ref, *refs):
    chunks = len(groups)
    kernels, owners, cell_rows, paired, held, parts, (out_ref,) = split(
        refs, count, chunks, chunks, chunks, chunks, chunks, 1
    )
    comps, width = out_ref.shape[1:]
    cosine, sine = angle_ref[:comps, 0:1], angle_ref[:comps, 1:2]
    for chunk in range(chunks):
        term = apply_owned(
            ids_ref, owners[chunk][...], paired[chunk][...], kernels, held[chunk][...].astype(F32)
        )
        term = term.astype(BF16).astype(F32)
        total, along, across, ice = (cell_rows[chunk][i : i + 1, :] for i in range(4))
        shrink = 1.0 / (1.0 + total)
        base = 1.0 - 0.5 * total * shrink
        energy = parts[chunk][:comps, :].astype(F32)
        forcing = jnp.maximum(cosine * along + sine * across, 0.0)
        result = energy * (base + forcing) + (0.2 * shrink) * term
        result = jnp.where(ice > 0, energy, result).astype(BF16)
        for k, row in enumerate(groups[chunk]):
            out_ref[row] = result[:, k * width : (k + 1) * width]


def finish(groups, found, owners, cell_rows, angles, paired, held, parts, width):
    ids, kernels = listed(found)
    comps = kernels[0].shape[0]
    operands = [angles, *kernels, *owners, *cell_rows, *paired, *held, *parts]
    return pl.pallas_call(
        functools.partial(finish_body, len(kernels), groups),
        out_shape=jax.ShapeDtypeStruct((sum(map(len, groups)), comps, width), BF16),
        in_specs=[SMEM] + [VMEM] * len(operands),
        out_specs=VMEM,
        compiler_params=params(),
        cost_estimate=transfer_cost(kernels, paired),
    )(ids, *operands)


def next_plane(value):
    return lax.ppermute(value, "plane", [(i, (i + 1) % PLANES) for i in range(PLANES)])


def boundaries(top, bottom):
    places = lax.axis_size("place")
    geo, count = ("plane", "place"), PLANES * places
    if places != 2:
        return (
            lax.ppermute(bottom, geo, [(i, i + 1) for i in range(count - 1)]),
            lax.ppermute(top, geo, [(i + 1, i) for i in range(count - 1)]),
        )
    first = lax.axis_index("place") == 0
    inside = lax.ppermute(jnp.where(first, bottom, top), "place", [(0, 1), (1, 0)])
    pairs = [(i, i + 1) for i in range(1, count - 1, 2)]
    outside = lax.ppermute(jnp.where(first, top, bottom), geo, pairs + [(j, i) for i, j in pairs])
    return inside, outside


def before_and_after(inside, outside):
    if lax.axis_size("place") != 2:
        return inside, outside
    first = lax.axis_index("place") == 0
    return jnp.where(first, outside, inside), jnp.where(first, inside, outside)


def with_partners(kernel, steps):
    count = lax.axis_size("place")
    plane, place = lax.axis_index("plane"), lax.axis_index("place")
    plane = lax.rem(plane + PLANES - steps, PLANES)
    found = [(kernel, plane * count + place)]
    for shift in range(1, count):
        pairs = [(i, (i + shift) % count) for i in range(count)]
        origin = lax.rem(place - shift + count, count)
        found.append((lax.ppermute(kernel, "place", pairs), plane * count + origin))
    return found


def send_spec(value, flip):
    return lax.ppermute(value, "spec", [(i, i ^ flip) for i in range(4)])


def per_device(
    spectrum,
    sea_map,
    depth_factor,
    wind_speed,
    wind_dir,
    ice_mask,
    owner_map,
    pair_kernel,
    transfer_kernel,
):
    comps, rows, width = spectrum.shape
    here = lax.axis_index("spec")

    own_rows = lax.dynamic_slice_in_dim(transfer_kernel[0], here * comps, comps, axis=0)
    one_back = next_plane(own_rows)
    sea = sea_map.astype(F32)
    top = spectrum[:, 0] * sea_map[0].astype(BF16)
    bottom = spectrum[:, rows - 1] * sea_map[rows - 1].astype(BF16)
    halos = boundaries(top, bottom)
    x = spectrum.transpose(1, 0, 2)

    component = here * comps + jnp.arange(comps, dtype=jnp.int32)
    frequency = (component // NDIR).astype(F32)
    heading = 2.0 * math.pi * ((component % NDIR).astype(F32) + 0.5) / NDIR
    cosine, sine = jnp.cos(heading), jnp.sin(heading)
    gain = jnp.float32(1.1) ** (-0.5 * frequency)
    coef = jnp.stack(
        [
            0.7 * gain * jnp.abs(cosine),
            0.7 * gain * jnp.abs(sine),
            (cosine > 0).astype(F32),
            (sine > 0).astype(F32),
        ],
        axis=1,
    )
    angles = jnp.stack([cosine, sine], axis=1)

    here_ref = jnp.reshape(here, (1,)).astype(jnp.int32)
    speed = 0.3 * wind_speed.astype(F32)
    along = speed * jnp.cos(wind_dir.astype(F32))
    across = speed * jnp.sin(wind_dir.astype(F32))
    wide = 3 * rows // 8
    one, two = 1 + wide, 1 + 2 * wide
    groups = [list(range(1, one)), list(range(one, two)), [0] + list(range(two, rows))]

    def cells_of(values):
        ends = jnp.concatenate([values[:1], values[two:]])
        return [v.reshape(1, -1) for v in (values[1:one], values[one:two], ends)]

    owners = cells_of(owner_map)
    extras = [cells_of(v) for v in (along, across, ice_mask.astype(F32))]

    def meet(part):
        return [send_spec(part, 1), send_spec(part, 2)]

    def pair_group(number, sets):
        paired, total = pair_up(here_ref, sets, pair_kernel)
        return paired, jnp.concatenate([total] + [extra[number] for extra in extras])

    none = jnp.zeros_like(top)
    parts = [
        propagate(group, x, none, none, sea, depth_factor, coef) for group in groups[:2]
    ]
    near = [meet(parts[0])]
    near[0], parts[1] = lax.optimization_barrier((near[0], parts[1]))
    near.append(meet(parts[1]))
    one_back, halos, near = lax.optimization_barrier((one_back, halos, near))

    two_back = next_plane(one_back)
    crossed = [send_spec(near[0][1], 1), send_spec(near[1][0], 2)]
    parts.append(
        propagate(groups[2], x, *before_and_after(*halos), sea, depth_factor, coef)
    )
    crossed, parts[2] = lax.optimization_barrier((crossed, parts[2]))
    near.append(meet(parts[2]))
    paired, cell_rows = [None] * 3, [None] * 3
    for i in range(2):
        paired[i], cell_rows[i] = pair_group(i, [parts[i], *near[i], crossed[i]])
    found = with_partners(own_rows, 0) + with_partners(one_back, 1)
    two_back, near, paired[:2] = lax.optimization_barrier((two_back, near, paired[:2]))

    three_back = next_plane(two_back)
    half = parts[2].shape[1] // 2
    crossed_last = [send_spec(near[2][1][:, :half], 1), send_spec(near[2][0][:, half:], 2)]
    held = transfer(found, owners[:2], paired[:2], None)
    held, crossed_last = lax.optimization_barrier((held, crossed_last))
    paired[2], cell_rows[2] = pair_group(2, [parts[2], *near[2], *crossed_last])
    later = with_partners(two_back, 2)
    held = transfer(later, owners[:2], paired[:2], held)
    held += transfer(found + later, owners[2:], paired[2:], None)
    three_back, held = lax.optimization_barrier((three_back, held))
    last = with_partners(three_back, 3)
    held = transfer(last[:-1], owners, paired, held)
    out = finish(groups, last[-1:], owners, cell_rows, angles, paired, held, parts, width)
    return out.transpose(1, 0, 2)


def solution(mesh):
    spec, geo = mesh.shape["spec"], mesh.shape["geo"]
    split = Mesh(
        mesh.devices.reshape(spec, PLANES, geo // PLANES), ("spec", "plane", "place")
    )
    tiles = ("plane", "place")
    placed = (
        P("spec", tiles, None),
        P(tiles, None),
        P(tiles, None),
        P(tiles, None),
        P(tiles, None),
        P(tiles, None),
        P(tiles, None),
        P(),
        P(tiles, None, None),
    )
    return jax.shard_map(
        per_device, mesh=split, in_specs=placed, out_specs=P("spec", tiles, None), check_vma=False
    )
```

```python
import functools
import math

import jax
import jax.numpy as jnp
from jax import lax
from jax.experimental import pallas as pl
from jax.experimental.pallas import tpu as pltpu
from jax.sharding import Mesh
from jax.sharding import PartitionSpec as P

NDIR = 36
PLANES = 4
SUB = 16
ANY = pl.BlockSpec(memory_space=pl.ANY)
VMEM = pl.BlockSpec(memory_space=pltpu.VMEM)
SMEM = pl.BlockSpec(memory_space=pltpu.SMEM)
BF16 = jnp.bfloat16
F32 = jnp.float32


def params(mib):
    return pltpu.CompilerParams(vmem_limit_bytes=mib * 2**20)


def places_of(rank, count):
    cells = rank.shape[1]
    kind = lax.broadcasted_iota(jnp.int32, (count, cells), 0)
    mine = (kind == rank).astype(F32)
    first = lax.broadcasted_iota(jnp.int32, (cells, cells), 0)
    second = lax.broadcasted_iota(jnp.int32, (cells, cells), 1)
    earlier = (first < second).astype(F32).astype(BF16)
    before = jnp.dot(mine.astype(BF16), earlier, preferred_element_type=F32)
    number = jnp.sum(mine, axis=1, keepdims=True)
    lower = (kind < rank).astype(F32)
    return jnp.sum(mine * before + lower * number, axis=0, keepdims=True)


def moves(place):
    cells = place.shape[1]
    target = lax.broadcasted_iota(jnp.int32, (cells, cells), 0)
    return (target == place.astype(jnp.int32)).astype(F32).astype(BF16)


def put_in_order(values, matrix):
    return lax.dot_general(
        values, matrix, (((1,), (1,)), ((), ())), preferred_element_type=F32
    )


def cells_of(values, rows):
    return jnp.concatenate([values[row : row + 1, :] for row in rows], axis=1)


def propagate_kernel(
    wanted,
    count,
    x_ref,
    west_ref,
    east_ref,
    sea_ref,
    depth_ref,
    coef_ref,
    rank_ref,
    sorted_ref,
    place_ref,
    out_ref,
):
    rows, comps, width = x_ref.shape

    def tile(at, height):
        lane = lax.broadcasted_iota(jnp.int32, (height, width), 1)
        coef = coef_ref[at, :]
        gain_x, gain_y, pos_x, pos_y = (
            jnp.broadcast_to(coef[:, i : i + 1], (height, width)) for i in range(4)
        )
        from_west, from_south = pos_x > 0, pos_y > 0
        first, last = lane == 0, lane == width - 1
        known = {}

        def masked(row):
            if row not in known:
                if row < 0:
                    known[row] = west_ref[at, :].astype(F32)
                elif row == rows:
                    known[row] = east_ref[at, :].astype(F32)
                else:
                    known[row] = x_ref[row, at, :].astype(F32) * sea_ref[row : row + 1, :]
            return known[row]

        for k, row in enumerate(wanted):
            west, centre, east = masked(row - 1), masked(row), masked(row + 1)
            upwind_x = jnp.where(from_west, west, east)
            south = jnp.where(first, 0.0, pltpu.roll(centre, 1, 1))
            north = jnp.where(last, 0.0, pltpu.roll(centre, width - 1, 1))
            upwind_y = jnp.where(from_south, south, north)
            depth = depth_ref[row : row + 1, :]
            moved = (
                centre
                - gain_x * depth * (centre - upwind_x)
                - gain_y * depth * (centre - upwind_y)
            )
            out_ref[at, k * width : (k + 1) * width] = (
                moved * sea_ref[row : row + 1, :]
            ).astype(BF16)

    def body(step, carry):
        tile(pl.ds(pl.multiple_of(step * SUB, SUB), SUB), SUB)
        return carry

    whole = comps // SUB
    lax.fori_loop(0, whole, body, 0)
    if comps % SUB:
        spare = out_ref.shape[0] - whole * SUB
        out_ref[whole * SUB :, :] = jnp.zeros((spare, out_ref.shape[1]), BF16)
        tile(slice(whole * SUB, comps), comps - whole * SUB)
    place = places_of(cells_of(rank_ref, wanted), count)
    place_ref[...] = place
    sorted_ref[...] = put_in_order(out_ref[...], moves(place)).astype(BF16)


def propagate(wanted, count, x, west, east, sea, depth, coef, rank_map):
    comps, width = x.shape[1:]
    padded = -(-comps // SUB) * SUB
    cells = len(wanted) * width
    return pl.pallas_call(
        functools.partial(propagate_kernel, wanted, count),
        out_shape=[
            jax.ShapeDtypeStruct((padded, cells), BF16),
            jax.ShapeDtypeStruct((1, cells), F32),
        ],
        in_specs=[VMEM] * 7,
        out_specs=[VMEM] * 2,
        scratch_shapes=[pltpu.VMEM((padded, cells), BF16)],
        compiler_params=params(20),
        cost_estimate=pl.CostEstimate(
            flops=2 * comps * cells, bytes_accessed=comps * cells, transcendentals=0
        ),
    )(x, west, east, sea, depth, coef, rank_map)


def split(refs, *sizes):
    out, at = [], 0
    for size in sizes:
        out.append(refs[at : at + size])
        at += size
    return out


def pair_body(tile, sizes, here_ref, *refs):
    groups = len(sizes)
    *parts, (pair_ref,), paired, totals, wholes = split(refs, *sizes, 1, groups, groups, groups)
    step = pl.program_id(0)
    comps = wholes[0].shape[0]
    some = comps // 4

    @pl.when(step == 0)
    def _():
        for here in range(4):

            @pl.when(here_ref[0] == here)
            def _(here=here):
                for pieces, whole in zip(parts, wholes):
                    for flip, piece in enumerate(pieces):
                        at = (here ^ flip) * some
                        whole[at : at + some, :] = piece[:some, :]

        for total, whole in zip(totals, wholes):
            total[...] = jnp.sum(whole[...].astype(F32), axis=0, keepdims=True) / comps

    for out_ref, whole in zip(paired, wholes):
        coupled = jnp.dot(pair_ref[...], whole[...], preferred_element_type=F32)
        own = whole[pl.ds(pl.multiple_of(step * tile, SUB), tile), :]
        out_ref[...] = (own.astype(F32) * coupled).astype(BF16)


def pair_up(here, groups, pair, tile=432):
    comps = pair.shape[0]
    sizes = [len(group) for group in groups]
    cells = [group[0].shape[1] for group in groups]
    flat = sum(groups, [])
    specs = [
        pl.BlockSpec(part.shape, lambda i: (0, 0), pipeline_mode=pl.Buffered(1)) for part in flat
    ]
    out = pl.pallas_call(
        functools.partial(pair_body, tile, sizes),
        grid=(comps // tile,),
        out_shape=[jax.ShapeDtypeStruct((comps, n), BF16) for n in cells]
        + [jax.ShapeDtypeStruct((1, n), F32) for n in cells],
        in_specs=[SMEM] + specs + [pl.BlockSpec((tile, comps), lambda i: (i, 0))],
        out_specs=[pl.BlockSpec((tile, n), lambda i: (i, 0)) for n in cells]
        + [pl.BlockSpec((1, n), lambda i: (0, 0)) for n in cells],
        scratch_shapes=[pltpu.VMEM((comps, n), BF16) for n in cells],
        compiler_params=params(20),
        cost_estimate=pl.CostEstimate(
            flops=comps * comps * sum(cells) // 4,
            bytes_accessed=comps * comps // 4,
            transcendentals=0,
        ),
    )(here, *flat, pair)
    return list(out[: len(groups)]), list(out[len(groups) :])


def apply_ranks(bounds_ref, at, which, paired, kernels, out, wide=256):
    cells = out.shape[1]
    for rank, kernel in which:
        begin, end = bounds_ref[at + rank], bounds_ref[at + rank + 1]
        for column in range(0, cells, wide):
            here = slice(column, column + wide)

            @pl.when((begin < column + wide) & (end > column))
            def _(here=here, column=column, kernel=kernel, begin=begin, end=end):
                term = jnp.dot(kernels[kernel][...], paired[:, here], preferred_element_type=F32)
                number = column + lax.broadcasted_iota(jnp.int32, term.shape, 1)
                mine = (number >= begin) & (number < end)
                out[:, here] = jnp.where(mine, term, out[:, here].astype(F32)).astype(BF16)


def product_cost(kernels, paired):
    flops = len(kernels) * kernels[0].size * sum(p.shape[1] for p in paired)
    moved = 2 * (len(kernels) * kernels[0].size + sum(p.size for p in paired))
    return pl.CostEstimate(flops=flops // 8, bytes_accessed=moved // 8, transcendentals=0)


def transfer_body(uses, strides, kept, bounds_ref, *refs):
    count, chunks = 1 + max(k for use in uses for _, k in use), len(uses)
    kernels, paired, held, outs, (mark,) = split(refs, count, chunks, len(kept), chunks, 1)
    mark[...] = jnp.zeros(mark.shape, F32)
    for chunk, out_ref in enumerate(outs):
        if chunk in kept:
            out_ref[...] = held[kept.index(chunk)][...]
        else:
            out_ref[...] = jnp.zeros(out_ref.shape, BF16)
        apply_ranks(bounds_ref, strides[chunk], uses[chunk], paired[chunk], kernels, out_ref)


def transfer(kernels, uses, strides, bounds, paired, held):
    kept = [i for i, value in enumerate(held) if value is not None]
    operands = [*kernels, *paired, *(held[i] for i in kept)]
    shapes = [jax.ShapeDtypeStruct((kernels[0].shape[0], p.shape[1]), BF16) for p in paired]
    shapes.append(jax.ShapeDtypeStruct((8, 128), F32))
    *held, mark = pl.pallas_call(
        functools.partial(transfer_body, uses, strides, kept),
        out_shape=shapes,
        in_specs=[SMEM] + [VMEM] * len(operands),
        out_specs=[VMEM] * len(shapes),
        compiler_params=params(8),
        cost_estimate=product_cost(kernels, paired),
    )(bounds, *operands)
    return held, mark


def transfer_all(kernels, first, strides, bounds, paired, held, most=6):
    mark = None
    for at in range(0, len(kernels), most):
        some = kernels[at : at + most]
        use = [(first + at + k, k) for k in range(len(some))]
        held, mark = transfer(some, [use] * len(paired), strides, bounds, paired, held)
    return held, mark


def finish_body(
    count, first, groups, strides, bounds_ref, coef_ref, ice_ref, speed_ref, angle_ref, *refs
):
    chunks = len(groups)
    kernels, places, totals, paired, held, parts = split(
        refs, count, chunks, chunks, chunks, chunks, chunks
    )
    out_ref, *works = refs[len(refs) - 1 - chunks :]
    comps, width = out_ref.shape[1:]
    maps = [speed_ref[...].astype(F32), angle_ref[...].astype(F32), ice_ref[...].astype(F32)]
    cosine, sine = coef_ref[:, 4:5], coef_ref[:, 5:6]
    for chunk, rows in enumerate(groups):
        work = works[chunk]
        work[...] = held[chunk][...]
        which = [(first + k, k) for k in range(count)]
        apply_ranks(bounds_ref, strides[chunk], which, paired[chunk], kernels, work)
        matrix = moves(places[chunk][...])
        given = [cells_of(values, rows) for values in maps]
        given = jnp.concatenate(given + [jnp.zeros_like(given[0])] * 5, axis=0)
        given = put_in_order(given.astype(BF16), matrix)
        speed, angle, frozen = 0.3 * given[0:1], given[1:2], given[2:3] > 0.5
        along, across = speed * jnp.cos(angle), speed * jnp.sin(angle)
        total = totals[chunk][...]
        shrink = 1.0 / (1.0 + total)
        base = 1.0 - 0.5 * total * shrink
        energy = parts[chunk][:comps, :].astype(F32)
        forcing = jnp.maximum(cosine * along + sine * across, 0.0)
        result = energy * (base + forcing) + (0.2 * shrink) * work[...].astype(F32)
        result = jnp.where(frozen, energy, result).astype(BF16)
        result = jnp.dot(result, matrix, preferred_element_type=F32).astype(BF16)
        for k, row in enumerate(rows):
            out_ref[row] = result[:, k * width : (k + 1) * width]


def finish(
    kernels, first, groups, strides, bounds, coef, maps, places, totals, paired, held, parts, marks
):
    comps = kernels[0].shape[0]
    rows, width = maps[0].shape
    operands = [coef, *maps, *kernels, *places, *totals, *paired, *held, *parts]
    return pl.pallas_call(
        functools.partial(finish_body, len(kernels), first, groups, strides),
        out_shape=jax.ShapeDtypeStruct((rows, comps, width), BF16),
        in_specs=[SMEM] + [VMEM] * len(operands) + [ANY] * len(marks),
        out_specs=VMEM,
        scratch_shapes=[pltpu.VMEM(value.shape, BF16) for value in held],
        compiler_params=params(20),
        cost_estimate=product_cost(kernels, paired),
    )(bounds, *operands, *marks)


def next_plane(value):
    return lax.ppermute(value, "plane", [(i, (i + 1) % PLANES) for i in range(PLANES)])


def boundaries(top, bottom):
    places = lax.axis_size("place")
    geo, count = ("plane", "place"), PLANES * places
    if places != 2:
        return (
            lax.ppermute(bottom, geo, [(i, i + 1) for i in range(count - 1)]),
            lax.ppermute(top, geo, [(i + 1, i) for i in range(count - 1)]),
        )
    first = lax.axis_index("place") == 0
    inside = lax.ppermute(jnp.where(first, bottom, top), "place", [(0, 1), (1, 0)])
    pairs = [(i, i + 1) for i in range(1, count - 1, 2)]
    outside = lax.ppermute(jnp.where(first, top, bottom), geo, pairs + [(j, i) for i, j in pairs])
    return inside, outside


def before_and_after(inside, outside):
    if lax.axis_size("place") != 2:
        return inside, outside
    first = lax.axis_index("place") == 0
    return jnp.where(first, outside, inside), jnp.where(first, inside, outside)


def with_partners(kernel):
    count = lax.axis_size("place")
    found = [kernel]
    for shift in range(1, count):
        pairs = [(i, (i + shift) % count) for i in range(count)]
        found.append(lax.ppermute(kernel, "place", pairs))
    return found


def ranks_of(owner_map):
    count = lax.axis_size("place")
    plane, place = lax.axis_index("plane"), lax.axis_index("place")
    steps = lax.rem(plane + PLANES - owner_map // count, PLANES)
    shift = lax.rem(place + count - lax.rem(owner_map, count), count)
    return steps * count + shift


def send_spec(value, flip):
    return lax.ppermute(value, "spec", [(i, i ^ flip) for i in range(4)])


def per_device(
    spectrum,
    sea_map,
    depth_factor,
    wind_speed,
    wind_dir,
    ice_mask,
    owner_map,
    pair_kernel,
    transfer_kernel,
):
    comps, rows, width = spectrum.shape
    here = lax.axis_index("spec")

    own_rows = lax.dynamic_slice_in_dim(transfer_kernel[0], here * comps, comps, axis=0)
    one_back = next_plane(own_rows)
    sea = sea_map.astype(F32)
    top = spectrum[:, 0] * sea_map[0].astype(BF16)
    bottom = spectrum[:, rows - 1] * sea_map[rows - 1].astype(BF16)
    halos = boundaries(top, bottom)
    x = spectrum.transpose(1, 0, 2)

    component = here * comps + jnp.arange(comps, dtype=jnp.int32)
    frequency = (component // NDIR).astype(F32)
    heading = 2.0 * math.pi * ((component % NDIR).astype(F32) + 0.5) / NDIR
    cosine, sine = jnp.cos(heading), jnp.sin(heading)
    gain = jnp.float32(1.1) ** (-0.5 * frequency)
    coef = jnp.stack(
        [
            0.7 * gain * jnp.abs(cosine),
            0.7 * gain * jnp.abs(sine),
            (cosine > 0).astype(F32),
            (sine > 0).astype(F32),
            cosine,
            sine,
        ],
        axis=1,
    )

    here_ref = jnp.reshape(here, (1,)).astype(jnp.int32)
    wide = 3 * rows // 8
    one, two = 1 + wide, 1 + 2 * wide
    groups = [list(range(1, one)), list(range(one, two)), [0] + list(range(two, rows))]

    def meet(part):
        return [send_spec(part, 1), send_spec(part, 2)]

    count = lax.axis_size("place")
    owners = PLANES * count
    rank_map = ranks_of(owner_map)
    kinds = jnp.arange(owners + 1, dtype=jnp.int32)
    bounds = []
    for group in groups:
        ranks = jnp.concatenate([rank_map[row] for row in group])
        bounds.append(jnp.sum((ranks[None, :] < kinds[:, None]).astype(jnp.int32), axis=1))
    bounds = jnp.concatenate(bounds)
    strides = [i * (owners + 1) for i in range(len(groups))]

    def move_rows(group, west, east):
        return propagate(
            group, owners, x, west, east, sea, depth_factor, coef, rank_map
        )

    none = jnp.zeros_like(top)
    parts, places = zip(*(move_rows(group, none, none) for group in groups[:2]))
    parts, places = list(parts), list(places)
    near = [meet(parts[0])]
    near[0], sent = lax.optimization_barrier((near[0], parts[1]))
    near.append(meet(sent))
    one_back, halos, near = lax.optimization_barrier((one_back, halos, near))

    two_back = next_plane(one_back)
    crossed = [send_spec(near[0][1], 1), send_spec(near[1][0], 2)]
    part, place = move_rows(groups[2], *before_and_after(*halos))
    parts.append(part)
    places.append(place)
    crossed, sent = lax.optimization_barrier((crossed, parts[2]))
    near.append(meet(sent))
    found = with_partners(own_rows) + with_partners(one_back)
    paired, totals = pair_up(
        here_ref, [[parts[i], *near[i], crossed[i]] for i in range(2)], pair_kernel
    )
    two_back, near[2], totals = lax.optimization_barrier((two_back, near[2], totals))

    three_back = next_plane(two_back)
    last_cross = send_spec(near[2][1], 1)
    held, mark = transfer_all(found, 0, strides[:2], bounds, paired, [None] * 2)
    last_cross, mark = lax.optimization_barrier((last_cross, mark))
    more, total = pair_up(here_ref, [[parts[2], *near[2], last_cross]], pair_kernel)
    paired, totals = paired + more, totals + total
    later = with_partners(two_back)
    if 3 * count <= 6:
        kernels = later + found
        some = [(2 * count + k, k) for k in range(count)]
        every = some + [(k, count + k) for k in range(2 * count)]
        held, other = transfer(
            kernels, [some, some, every], strides, bounds, paired, [*held, None]
        )
    else:
        more, _ = transfer_all(found, 0, strides[2:], bounds, paired[2:], [None])
        held, other = transfer_all(later, 2 * count, strides, bounds, paired, [*held, *more])
    three_back, other = lax.optimization_barrier((three_back, other))
    last = with_partners(three_back)
    if last[:-1]:
        held, _ = transfer_all(last[:-1], 3 * count, strides, bounds, paired, held)
    maps = [ice_mask, wind_speed, wind_dir]
    out = finish(
        last[-1:],
        owners - 1,
        groups,
        strides,
        bounds,
        coef,
        maps,
        places,
        totals,
        paired,
        held,
        parts,
        [mark, other],
    )
    return out.transpose(1, 0, 2)


def solution(mesh):
    spec, geo = mesh.shape["spec"], mesh.shape["geo"]
    split = Mesh(
        mesh.devices.reshape(spec, PLANES, geo // PLANES), ("spec", "plane", "place")
    )
    tiles = ("plane", "place")
    placed = (
        P("spec", tiles, None),
        P(tiles, None),
        P(tiles, None),
        P(tiles, None),
        P(tiles, None),
        P(tiles, None),
        P(tiles, None),
        P(),
        P(tiles, None, None),
    )
    return jax.shard_map(
        per_device, mesh=split, in_specs=placed, out_specs=P("spec", tiles, None), check_vma=False
    )
```

```python
import functools
import math

import jax
import jax.numpy as jnp
from jax import lax
from jax.experimental import pallas as pl
from jax.experimental.pallas import tpu as pltpu
from jax.sharding import Mesh
from jax.sharding import PartitionSpec as P

NDIR = 36
PLANES = 4
SUB = 16
ANY = pl.BlockSpec(memory_space=pl.ANY)
VMEM = pl.BlockSpec(memory_space=pltpu.VMEM)
SMEM = pl.BlockSpec(memory_space=pltpu.SMEM)
BF16 = jnp.bfloat16
F32 = jnp.float32


def params(mib):
    return pltpu.CompilerParams(vmem_limit_bytes=mib * 2**20)


def places_of(rank, count):
    cells = rank.shape[1]
    kind = lax.broadcasted_iota(jnp.int32, (count, cells), 0)
    mine = (kind == rank).astype(F32)
    first = lax.broadcasted_iota(jnp.int32, (cells, cells), 0)
    second = lax.broadcasted_iota(jnp.int32, (cells, cells), 1)
    earlier = (first < second).astype(F32).astype(BF16)
    before = jnp.dot(mine.astype(BF16), earlier, preferred_element_type=F32)
    number = jnp.sum(mine, axis=1, keepdims=True)
    lower = (kind < rank).astype(F32)
    return jnp.sum(mine * before + lower * number, axis=0, keepdims=True)


def moves(place):
    cells = place.shape[1]
    target = lax.broadcasted_iota(jnp.int32, (cells, cells), 0)
    return (target == place.astype(jnp.int32)).astype(F32).astype(BF16)


def put_in_order(values, matrix):
    return lax.dot_general(
        values, matrix, (((1,), (1,)), ((), ())), preferred_element_type=F32
    )


def cells_of(values, rows):
    return jnp.concatenate([values[row : row + 1, :] for row in rows], axis=1)


def propagate_kernel(
    wanted,
    count,
    x_ref,
    west_ref,
    east_ref,
    sea_ref,
    depth_ref,
    coef_ref,
    rank_ref,
    sorted_ref,
    place_ref,
    out_ref,
):
    rows, comps, width = x_ref.shape

    def tile(at, height):
        lane = lax.broadcasted_iota(jnp.int32, (height, width), 1)
        coef = coef_ref[at, :]
        gain_x, gain_y, pos_x, pos_y = (
            jnp.broadcast_to(coef[:, i : i + 1], (height, width)) for i in range(4)
        )
        from_west, from_south = pos_x > 0, pos_y > 0
        first, last = lane == 0, lane == width - 1
        known = {}

        def masked(row):
            if row not in known:
                if row < 0:
                    known[row] = west_ref[at, :].astype(F32)
                elif row == rows:
                    known[row] = east_ref[at, :].astype(F32)
                else:
                    known[row] = x_ref[row, at, :].astype(F32) * sea_ref[row : row + 1, :]
            return known[row]

        for k, row in enumerate(wanted):
            west, centre, east = masked(row - 1), masked(row), masked(row + 1)
            upwind_x = jnp.where(from_west, west, east)
            south = jnp.where(first, 0.0, pltpu.roll(centre, 1, 1))
            north = jnp.where(last, 0.0, pltpu.roll(centre, width - 1, 1))
            upwind_y = jnp.where(from_south, south, north)
            depth = depth_ref[row : row + 1, :]
            moved = (
                centre
                - gain_x * depth * (centre - upwind_x)
                - gain_y * depth * (centre - upwind_y)
            )
            out_ref[at, k * width : (k + 1) * width] = (
                moved * sea_ref[row : row + 1, :]
            ).astype(BF16)

    def body(step, carry):
        tile(pl.ds(pl.multiple_of(step * SUB, SUB), SUB), SUB)
        return carry

    whole = comps // SUB
    lax.fori_loop(0, whole, body, 0)
    if comps % SUB:
        spare = out_ref.shape[0] - whole * SUB
        out_ref[whole * SUB :, :] = jnp.zeros((spare, out_ref.shape[1]), BF16)
        tile(slice(whole * SUB, comps), comps - whole * SUB)
    place = places_of(cells_of(rank_ref, wanted), count)
    place_ref[...] = place
    sorted_ref[...] = put_in_order(out_ref[...], moves(place)).astype(BF16)


def propagate(wanted, count, x, west, east, sea, depth, coef, rank_map):
    comps, width = x.shape[1:]
    padded = -(-comps // SUB) * SUB
    cells = len(wanted) * width
    return pl.pallas_call(
        functools.partial(propagate_kernel, wanted, count),
        out_shape=[
            jax.ShapeDtypeStruct((padded, cells), BF16),
            jax.ShapeDtypeStruct((1, cells), F32),
        ],
        in_specs=[VMEM] * 7,
        out_specs=[VMEM] * 2,
        scratch_shapes=[pltpu.VMEM((padded, cells), BF16)],
        compiler_params=params(20),
        cost_estimate=pl.CostEstimate(
            flops=2 * comps * cells, bytes_accessed=comps * cells, transcendentals=0
        ),
    )(x, west, east, sea, depth, coef, rank_map)


def split(refs, *sizes):
    out, at = [], 0
    for size in sizes:
        out.append(refs[at : at + size])
        at += size
    return out


def pair_body(tile, sizes, here_ref, *refs):
    groups = len(sizes)
    *parts, (pair_ref,), paired, totals, wholes = split(refs, *sizes, 1, groups, groups, groups)
    step = pl.program_id(0)
    comps = wholes[0].shape[0]
    some = comps // 4

    @pl.when(step == 0)
    def _():
        for here in range(4):

            @pl.when(here_ref[0] == here)
            def _(here=here):
                for pieces, whole in zip(parts, wholes):
                    for flip, piece in enumerate(pieces):
                        at = (here ^ flip) * some
                        whole[at : at + some, :] = piece[:some, :]

        for total, whole in zip(totals, wholes):
            total[...] = jnp.sum(whole[...].astype(F32), axis=0, keepdims=True) / comps

    for out_ref, whole in zip(paired, wholes):
        coupled = jnp.dot(pair_ref[...], whole[...], preferred_element_type=F32)
        own = whole[pl.ds(pl.multiple_of(step * tile, SUB), tile), :]
        out_ref[...] = (own.astype(F32) * coupled).astype(BF16)


def pair_up(here, groups, pair, tile=432):
    comps = pair.shape[0]
    sizes = [len(group) for group in groups]
    cells = [group[0].shape[1] for group in groups]
    flat = sum(groups, [])
    specs = [
        pl.BlockSpec(part.shape, lambda i: (0, 0), pipeline_mode=pl.Buffered(1)) for part in flat
    ]
    out = pl.pallas_call(
        functools.partial(pair_body, tile, sizes),
        grid=(comps // tile,),
        out_shape=[jax.ShapeDtypeStruct((comps, n), BF16) for n in cells]
        + [jax.ShapeDtypeStruct((1, n), F32) for n in cells],
        in_specs=[SMEM] + specs + [pl.BlockSpec((tile, comps), lambda i: (i, 0))],
        out_specs=[pl.BlockSpec((tile, n), lambda i: (i, 0)) for n in cells]
        + [pl.BlockSpec((1, n), lambda i: (0, 0)) for n in cells],
        scratch_shapes=[pltpu.VMEM((comps, n), BF16) for n in cells],
        compiler_params=params(20),
        cost_estimate=pl.CostEstimate(
            flops=comps * comps * sum(cells) // 4,
            bytes_accessed=comps * comps // 4,
            transcendentals=0,
        ),
    )(here, *flat, pair)
    return list(out[: len(groups)]), list(out[len(groups) :])


def apply_ranks(bounds_ref, at, which, paired, kernels, out, wide=256):
    cells = out.shape[1]
    for rank, kernel in which:
        begin, end = bounds_ref[at + rank], bounds_ref[at + rank + 1]
        for column in range(0, cells, wide):
            here = slice(column, column + wide)

            @pl.when((begin < column + wide) & (end > column))
            def _(here=here, column=column, kernel=kernel, begin=begin, end=end):
                term = jnp.dot(kernels[kernel][...], paired[:, here], preferred_element_type=F32)
                number = column + lax.broadcasted_iota(jnp.int32, term.shape, 1)
                mine = (number >= begin) & (number < end)
                out[:, here] = jnp.where(mine, term, out[:, here].astype(F32)).astype(BF16)


def product_cost(kernels, paired):
    flops = len(kernels) * kernels[0].size * sum(p.shape[1] for p in paired)
    moved = 2 * (len(kernels) * kernels[0].size + sum(p.size for p in paired))
    return pl.CostEstimate(flops=flops // 8, bytes_accessed=moved // 8, transcendentals=0)


def transfer_body(uses, strides, kept, bounds_ref, *refs):
    count, chunks = 1 + max(k for use in uses for _, k in use), len(uses)
    kernels, paired, held, outs, (mark,) = split(refs, count, chunks, len(kept), chunks, 1)
    mark[...] = jnp.zeros(mark.shape, F32)
    for chunk, out_ref in enumerate(outs):
        if chunk in kept:
            out_ref[...] = held[kept.index(chunk)][...]
        else:
            out_ref[...] = jnp.zeros(out_ref.shape, BF16)
        apply_ranks(bounds_ref, strides[chunk], uses[chunk], paired[chunk], kernels, out_ref)


def transfer(kernels, uses, strides, bounds, paired, held):
    kept = [i for i, value in enumerate(held) if value is not None]
    operands = [*kernels, *paired, *(held[i] for i in kept)]
    shapes = [jax.ShapeDtypeStruct((kernels[0].shape[0], p.shape[1]), BF16) for p in paired]
    shapes.append(jax.ShapeDtypeStruct((8, 128), F32))
    *held, mark = pl.pallas_call(
        functools.partial(transfer_body, uses, strides, kept),
        out_shape=shapes,
        in_specs=[SMEM] + [VMEM] * len(operands),
        out_specs=[VMEM] * len(shapes),
        compiler_params=params(8),
        cost_estimate=product_cost(kernels, paired),
    )(bounds, *operands)
    return held, mark


def transfer_all(kernels, first, strides, bounds, paired, held, most=6):
    mark = None
    for at in range(0, len(kernels), most):
        some = kernels[at : at + most]
        use = [(first + at + k, k) for k in range(len(some))]
        held, mark = transfer(some, [use] * len(paired), strides, bounds, paired, held)
    return held, mark


def finish_body(
    count, first, groups, strides, bounds_ref, coef_ref, ice_ref, speed_ref, angle_ref, *refs
):
    chunks = len(groups)
    kernels, places, totals, paired, held, parts = split(
        refs, count, chunks, chunks, chunks, chunks, chunks
    )
    out_ref, *works = refs[len(refs) - 1 - chunks :]
    comps, width = out_ref.shape[1:]
    maps = [speed_ref[...].astype(F32), angle_ref[...].astype(F32), ice_ref[...].astype(F32)]
    cosine, sine = coef_ref[:, 4:5], coef_ref[:, 5:6]
    for chunk, rows in enumerate(groups):
        work = works[chunk]
        work[...] = held[chunk][...]
        which = [(first + k, k) for k in range(count)]
        apply_ranks(bounds_ref, strides[chunk], which, paired[chunk], kernels, work)
        matrix = moves(places[chunk][...])
        given = [cells_of(values, rows) for values in maps]
        given = jnp.concatenate(given + [jnp.zeros_like(given[0])] * 5, axis=0)
        given = put_in_order(given.astype(BF16), matrix)
        speed, angle, frozen = 0.3 * given[0:1], given[1:2], given[2:3] > 0.5
        along, across = speed * jnp.cos(angle), speed * jnp.sin(angle)
        total = totals[chunk][...]
        shrink = 1.0 / (1.0 + total)
        base = 1.0 - 0.5 * total * shrink
        energy = parts[chunk][:comps, :].astype(F32)
        forcing = jnp.maximum(cosine * along + sine * across, 0.0)
        result = energy * (base + forcing) + (0.2 * shrink) * work[...].astype(F32)
        result = jnp.where(frozen, energy, result).astype(BF16)
        result = jnp.dot(result, matrix, preferred_element_type=F32).astype(BF16)
        for k, row in enumerate(rows):
            out_ref[row] = result[:, k * width : (k + 1) * width]


def finish(
    kernels, first, groups, strides, bounds, coef, maps, places, totals, paired, held, parts, marks
):
    comps = kernels[0].shape[0]
    rows, width = maps[0].shape
    operands = [coef, *maps, *kernels, *places, *totals, *paired, *held, *parts]
    return pl.pallas_call(
        functools.partial(finish_body, len(kernels), first, groups, strides),
        out_shape=jax.ShapeDtypeStruct((rows, comps, width), BF16),
        in_specs=[SMEM] + [VMEM] * len(operands) + [ANY] * len(marks),
        out_specs=VMEM,
        scratch_shapes=[pltpu.VMEM(value.shape, BF16) for value in held],
        compiler_params=params(20),
        cost_estimate=product_cost(kernels, paired),
    )(bounds, *operands, *marks)


def next_plane(value):
    return lax.ppermute(value, "plane", [(i, (i + 1) % PLANES) for i in range(PLANES)])


def boundaries(top, bottom):
    places = lax.axis_size("place")
    geo, count = ("plane", "place"), PLANES * places
    if places != 2:
        return (
            lax.ppermute(bottom, geo, [(i, i + 1) for i in range(count - 1)]),
            lax.ppermute(top, geo, [(i + 1, i) for i in range(count - 1)]),
        )
    first = lax.axis_index("place") == 0
    inside = lax.ppermute(jnp.where(first, bottom, top), "place", [(0, 1), (1, 0)])
    pairs = [(i, i + 1) for i in range(1, count - 1, 2)]
    outside = lax.ppermute(jnp.where(first, top, bottom), geo, pairs + [(j, i) for i, j in pairs])
    return inside, outside


def before_and_after(inside, outside):
    if lax.axis_size("place") != 2:
        return inside, outside
    first = lax.axis_index("place") == 0
    return jnp.where(first, outside, inside), jnp.where(first, inside, outside)


def with_partners(kernel):
    count = lax.axis_size("place")
    found = [kernel]
    for shift in range(1, count):
        pairs = [(i, (i + shift) % count) for i in range(count)]
        found.append(lax.ppermute(kernel, "place", pairs))
    return found


def ranks_of(owner_map):
    count = lax.axis_size("place")
    plane, place = lax.axis_index("plane"), lax.axis_index("place")
    steps = lax.rem(plane + PLANES - owner_map // count, PLANES)
    shift = lax.rem(place + count - lax.rem(owner_map, count), count)
    return steps * count + shift


def send_spec(value, flip):
    return lax.ppermute(value, "spec", [(i, i ^ flip) for i in range(4)])


def per_device(
    spectrum,
    sea_map,
    depth_factor,
    wind_speed,
    wind_dir,
    ice_mask,
    owner_map,
    pair_kernel,
    transfer_kernel,
):
    comps, rows, width = spectrum.shape
    here = lax.axis_index("spec")

    own_rows = lax.dynamic_slice_in_dim(transfer_kernel[0], here * comps, comps, axis=0)
    one_back = next_plane(own_rows)
    sea = sea_map.astype(F32)
    top = spectrum[:, 0] * sea_map[0].astype(BF16)
    bottom = spectrum[:, rows - 1] * sea_map[rows - 1].astype(BF16)
    halos = boundaries(top, bottom)
    x = spectrum.transpose(1, 0, 2)

    component = here * comps + jnp.arange(comps, dtype=jnp.int32)
    frequency = (component // NDIR).astype(F32)
    heading = 2.0 * math.pi * ((component % NDIR).astype(F32) + 0.5) / NDIR
    cosine, sine = jnp.cos(heading), jnp.sin(heading)
    gain = jnp.float32(1.1) ** (-0.5 * frequency)
    coef = jnp.stack(
        [
            0.7 * gain * jnp.abs(cosine),
            0.7 * gain * jnp.abs(sine),
            (cosine > 0).astype(F32),
            (sine > 0).astype(F32),
            cosine,
            sine,
        ],
        axis=1,
    )

    here_ref = jnp.reshape(here, (1,)).astype(jnp.int32)
    wide = 3 * rows // 8
    one, two = 1 + wide, 1 + 2 * wide
    groups = [list(range(1, one)), list(range(one, two)), [0] + list(range(two, rows))]

    def meet(part):
        return [send_spec(part, 1), send_spec(part, 2)]

    count = lax.axis_size("place")
    owners = PLANES * count
    rank_map = ranks_of(owner_map)
    kinds = jnp.arange(owners + 1, dtype=jnp.int32)
    bounds = []
    for group in groups:
        ranks = jnp.concatenate([rank_map[row] for row in group])
        bounds.append(jnp.sum((ranks[None, :] < kinds[:, None]).astype(jnp.int32), axis=1))
    bounds = jnp.concatenate(bounds)
    strides = [i * (owners + 1) for i in range(len(groups))]

    def move_rows(group, west, east):
        return propagate(
            group, owners, x, west, east, sea, depth_factor, coef, rank_map
        )

    none = jnp.zeros_like(top)
    parts, places = zip(*(move_rows(group, none, none) for group in groups[:2]))
    parts, places = list(parts), list(places)
    near = [meet(parts[0])]
    one_back, halos, near[0], sent = lax.optimization_barrier(
        (one_back, halos, near[0], parts[1])
    )

    two_back = next_plane(one_back)
    near.append(meet(sent))
    crossed = [send_spec(near[0][1], 1), send_spec(near[1][0], 2)]
    part, place = move_rows(groups[2], *before_and_after(*halos))
    parts.append(part)
    places.append(place)
    found = with_partners(own_rows) + with_partners(one_back)
    marks = [value[:8, :128] for value in (found[1], found[count + 1])]
    two_back, crossed, near[1], sent, marks = lax.optimization_barrier(
        (two_back, crossed, near[1], parts[2], marks)
    )
    near.append(meet(sent))
    paired, totals = pair_up(
        here_ref, [[parts[i], *near[i], crossed[i]] for i in range(2)], pair_kernel
    )

    three_back = next_plane(two_back)
    near[2], totals = lax.optimization_barrier((near[2], totals))
    last_cross = send_spec(near[2][1], 1)
    held, mark = transfer_all(found, 0, strides[:2], bounds, paired, [None] * 2)
    last_cross, mark = lax.optimization_barrier((last_cross, mark))
    more, total = pair_up(here_ref, [[parts[2], *near[2], last_cross]], pair_kernel)
    paired, totals = paired + more, totals + total
    later = with_partners(two_back)
    if 3 * count <= 6:
        kernels = later + found
        some = [(2 * count + k, k) for k in range(count)]
        every = some + [(k, count + k) for k in range(2 * count)]
        held, other = transfer(
            kernels, [some, some, every], strides, bounds, paired, [*held, None]
        )
    else:
        more, _ = transfer_all(found, 0, strides[2:], bounds, paired[2:], [None])
        held, other = transfer_all(later, 2 * count, strides, bounds, paired, [*held, *more])
    three_back, other = lax.optimization_barrier((three_back, other))
    last = with_partners(three_back)
    if last[:-1]:
        held, _ = transfer_all(last[:-1], 3 * count, strides, bounds, paired, held)
    maps = [ice_mask, wind_speed, wind_dir]
    out = finish(
        last[-1:],
        owners - 1,
        groups,
        strides,
        bounds,
        coef,
        maps,
        places,
        totals,
        paired,
        held,
        parts,
        [mark, other, *marks],
    )
    return out.transpose(1, 0, 2)


def solution(mesh):
    spec, geo = mesh.shape["spec"], mesh.shape["geo"]
    split = Mesh(
        mesh.devices.reshape(spec, PLANES, geo // PLANES), ("spec", "plane", "place")
    )
    tiles = ("plane", "place")
    placed = (
        P("spec", tiles, None),
        P(tiles, None),
        P(tiles, None),
        P(tiles, None),
        P(tiles, None),
        P(tiles, None),
        P(tiles, None),
        P(),
        P(tiles, None, None),
    )
    return jax.shard_map(
        per_device, mesh=split, in_specs=placed, out_specs=P("spec", tiles, None), check_vma=False
    )
```

```python
import functools
import math

import jax
import jax.numpy as jnp
from jax import lax
from jax.experimental import pallas as pl
from jax.experimental.pallas import tpu as pltpu
from jax.sharding import Mesh
from jax.sharding import PartitionSpec as P

NDIR = 36
PLANES = 4
SUB = 16
ANY = pl.BlockSpec(memory_space=pl.ANY)
VMEM = pl.BlockSpec(memory_space=pltpu.VMEM)
SMEM = pl.BlockSpec(memory_space=pltpu.SMEM)
BF16 = jnp.bfloat16
F32 = jnp.float32


def params(mib):
    return pltpu.CompilerParams(vmem_limit_bytes=mib * 2**20)


def places_of(rank, count):
    cells = rank.shape[1]
    kind = lax.broadcasted_iota(jnp.int32, (count, cells), 0)
    mine = (kind == rank).astype(F32)
    first = lax.broadcasted_iota(jnp.int32, (cells, cells), 0)
    second = lax.broadcasted_iota(jnp.int32, (cells, cells), 1)
    earlier = (first < second).astype(F32).astype(BF16)
    before = jnp.dot(mine.astype(BF16), earlier, preferred_element_type=F32)
    number = jnp.sum(mine, axis=1, keepdims=True)
    lower = (kind < rank).astype(F32)
    return jnp.sum(mine * before + lower * number, axis=0, keepdims=True)


def moves(place):
    cells = place.shape[1]
    target = lax.broadcasted_iota(jnp.int32, (cells, cells), 0)
    return (target == place.astype(jnp.int32)).astype(F32).astype(BF16)


def put_in_order(values, matrix):
    return lax.dot_general(
        values, matrix, (((1,), (1,)), ((), ())), preferred_element_type=F32
    )


def cells_of(values, rows):
    return jnp.concatenate([values[row : row + 1, :] for row in rows], axis=1)


def propagate_kernel(
    wanted,
    count,
    x_ref,
    west_ref,
    east_ref,
    sea_ref,
    depth_ref,
    coef_ref,
    rank_ref,
    sorted_ref,
    place_ref,
    out_ref,
):
    rows, comps, width = x_ref.shape

    def tile(at, height):
        lane = lax.broadcasted_iota(jnp.int32, (height, width), 1)
        coef = coef_ref[at, :]
        gain_x, gain_y, pos_x, pos_y = (
            jnp.broadcast_to(coef[:, i : i + 1], (height, width)) for i in range(4)
        )
        from_west, from_south = pos_x > 0, pos_y > 0
        first, last = lane == 0, lane == width - 1
        known = {}

        def masked(row):
            if row not in known:
                if row < 0:
                    known[row] = west_ref[at, :].astype(F32)
                elif row == rows:
                    known[row] = east_ref[at, :].astype(F32)
                else:
                    known[row] = x_ref[row, at, :].astype(F32) * sea_ref[row : row + 1, :]
            return known[row]

        for k, row in enumerate(wanted):
            west, centre, east = masked(row - 1), masked(row), masked(row + 1)
            upwind_x = jnp.where(from_west, west, east)
            south = jnp.where(first, 0.0, pltpu.roll(centre, 1, 1))
            north = jnp.where(last, 0.0, pltpu.roll(centre, width - 1, 1))
            upwind_y = jnp.where(from_south, south, north)
            depth = depth_ref[row : row + 1, :]
            moved = (
                centre
                - gain_x * depth * (centre - upwind_x)
                - gain_y * depth * (centre - upwind_y)
            )
            out_ref[at, k * width : (k + 1) * width] = (
                moved * sea_ref[row : row + 1, :]
            ).astype(BF16)

    def body(step, carry):
        tile(pl.ds(pl.multiple_of(step * SUB, SUB), SUB), SUB)
        return carry

    whole = comps // SUB
    lax.fori_loop(0, whole, body, 0)
    if comps % SUB:
        spare = out_ref.shape[0] - whole * SUB
        out_ref[whole * SUB :, :] = jnp.zeros((spare, out_ref.shape[1]), BF16)
        tile(slice(whole * SUB, comps), comps - whole * SUB)
    place = places_of(cells_of(rank_ref, wanted), count)
    place_ref[...] = place
    sorted_ref[...] = put_in_order(out_ref[...], moves(place)).astype(BF16)


def propagate(wanted, count, x, west, east, sea, depth, coef, rank_map):
    comps, width = x.shape[1:]
    padded = -(-comps // SUB) * SUB
    cells = len(wanted) * width
    return pl.pallas_call(
        functools.partial(propagate_kernel, wanted, count),
        out_shape=[
            jax.ShapeDtypeStruct((padded, cells), BF16),
            jax.ShapeDtypeStruct((1, cells), F32),
        ],
        in_specs=[VMEM] * 7,
        out_specs=[VMEM] * 2,
        scratch_shapes=[pltpu.VMEM((padded, cells), BF16)],
        compiler_params=params(20),
        cost_estimate=pl.CostEstimate(
            flops=2 * comps * cells, bytes_accessed=comps * cells, transcendentals=0
        ),
    )(x, west, east, sea, depth, coef, rank_map)


def split(refs, *sizes):
    out, at = [], 0
    for size in sizes:
        out.append(refs[at : at + size])
        at += size
    return out


def pair_body(tile, sizes, here_ref, *refs):
    groups = len(sizes)
    *parts, (pair_ref,), paired, totals, wholes = split(refs, *sizes, 1, groups, groups, groups)
    step = pl.program_id(0)
    comps = wholes[0].shape[0]
    some = comps // 4

    @pl.when(step == 0)
    def _():
        for here in range(4):

            @pl.when(here_ref[0] == here)
            def _(here=here):
                for pieces, whole in zip(parts, wholes):
                    for flip, piece in enumerate(pieces):
                        at = (here ^ flip) * some
                        whole[at : at + some, :] = piece[:some, :]

        for total, whole in zip(totals, wholes):
            total[...] = jnp.sum(whole[...].astype(F32), axis=0, keepdims=True) / comps

    for out_ref, whole in zip(paired, wholes):
        coupled = jnp.dot(pair_ref[...], whole[...], preferred_element_type=F32)
        own = whole[pl.ds(pl.multiple_of(step * tile, SUB), tile), :]
        out_ref[...] = (own.astype(F32) * coupled).astype(BF16)


def pair_up(here, groups, pair, tile=432):
    comps = pair.shape[0]
    sizes = [len(group) for group in groups]
    cells = [group[0].shape[1] for group in groups]
    flat = sum(groups, [])
    specs = [
        pl.BlockSpec(part.shape, lambda i: (0, 0), pipeline_mode=pl.Buffered(1)) for part in flat
    ]
    out = pl.pallas_call(
        functools.partial(pair_body, tile, sizes),
        grid=(comps // tile,),
        out_shape=[jax.ShapeDtypeStruct((comps, n), BF16) for n in cells]
        + [jax.ShapeDtypeStruct((1, n), F32) for n in cells],
        in_specs=[SMEM] + specs + [pl.BlockSpec((tile, comps), lambda i: (i, 0))],
        out_specs=[pl.BlockSpec((tile, n), lambda i: (i, 0)) for n in cells]
        + [pl.BlockSpec((1, n), lambda i: (0, 0)) for n in cells],
        scratch_shapes=[pltpu.VMEM((comps, n), BF16) for n in cells],
        compiler_params=params(20),
        cost_estimate=pl.CostEstimate(
            flops=comps * comps * sum(cells) // 4,
            bytes_accessed=comps * comps // 4,
            transcendentals=0,
        ),
    )(here, *flat, pair)
    return list(out[: len(groups)]), list(out[len(groups) :])


def apply_ranks(bounds_ref, at, which, paired, kernels, out, wide=256):
    cells = out.shape[1]
    for rank, kernel in which:
        begin, end = bounds_ref[at + rank], bounds_ref[at + rank + 1]
        for column in range(0, cells, wide):
            here = slice(column, column + wide)

            @pl.when((begin < column + wide) & (end > column))
            def _(here=here, column=column, kernel=kernel, begin=begin, end=end):
                term = jnp.dot(kernels[kernel][...], paired[:, here], preferred_element_type=F32)
                number = column + lax.broadcasted_iota(jnp.int32, term.shape, 1)
                mine = (number >= begin) & (number < end)
                out[:, here] = jnp.where(mine, term, out[:, here].astype(F32)).astype(BF16)


def product_cost(kernels, paired):
    flops = len(kernels) * kernels[0].size * sum(p.shape[1] for p in paired)
    moved = 2 * (len(kernels) * kernels[0].size + sum(p.size for p in paired))
    return pl.CostEstimate(flops=flops // 8, bytes_accessed=moved // 8, transcendentals=0)


def transfer_body(uses, strides, kept, bounds_ref, *refs):
    count, chunks = 1 + max(k for use in uses for _, k in use), len(uses)
    kernels, paired, held, outs, (mark,) = split(refs, count, chunks, len(kept), chunks, 1)
    mark[...] = jnp.zeros(mark.shape, F32)
    for chunk, out_ref in enumerate(outs):
        if chunk in kept:
            out_ref[...] = held[kept.index(chunk)][...]
        else:
            out_ref[...] = jnp.zeros(out_ref.shape, BF16)
        apply_ranks(bounds_ref, strides[chunk], uses[chunk], paired[chunk], kernels, out_ref)


def transfer(kernels, uses, strides, bounds, paired, held):
    kept = [i for i, value in enumerate(held) if value is not None]
    operands = [*kernels, *paired, *(held[i] for i in kept)]
    shapes = [jax.ShapeDtypeStruct((kernels[0].shape[0], p.shape[1]), BF16) for p in paired]
    shapes.append(jax.ShapeDtypeStruct((8, 128), F32))
    *held, mark = pl.pallas_call(
        functools.partial(transfer_body, uses, strides, kept),
        out_shape=shapes,
        in_specs=[SMEM] + [VMEM] * len(operands),
        out_specs=[VMEM] * len(shapes),
        compiler_params=params(8),
        cost_estimate=product_cost(kernels, paired),
    )(bounds, *operands)
    return held, mark


def transfer_all(kernels, first, strides, bounds, paired, held, most=6):
    mark = None
    for at in range(0, len(kernels), most):
        some = kernels[at : at + most]
        use = [(first + at + k, k) for k in range(len(some))]
        held, mark = transfer(some, [use] * len(paired), strides, bounds, paired, held)
    return held, mark


def finish_body(
    count, first, groups, strides, bounds_ref, coef_ref, ice_ref, speed_ref, angle_ref, *refs
):
    chunks = len(groups)
    kernels, places, totals, paired, held, parts = split(
        refs, count, chunks, chunks, chunks, chunks, chunks
    )
    out_ref, *works = refs[len(refs) - 1 - chunks :]
    comps, width = out_ref.shape[1:]
    maps = [speed_ref[...].astype(F32), angle_ref[...].astype(F32), ice_ref[...].astype(F32)]
    cosine, sine = coef_ref[:, 4:5], coef_ref[:, 5:6]
    for chunk, rows in enumerate(groups):
        work = works[chunk]
        work[...] = held[chunk][...]
        which = [(first + k, k) for k in range(count)]
        apply_ranks(bounds_ref, strides[chunk], which, paired[chunk], kernels, work)
        matrix = moves(places[chunk][...])
        given = [cells_of(values, rows) for values in maps]
        given = jnp.concatenate(given + [jnp.zeros_like(given[0])] * 5, axis=0)
        given = put_in_order(given.astype(BF16), matrix)
        speed, angle, frozen = 0.3 * given[0:1], given[1:2], given[2:3] > 0.5
        along, across = speed * jnp.cos(angle), speed * jnp.sin(angle)
        total = totals[chunk][...]
        shrink = 1.0 / (1.0 + total)
        base = 1.0 - 0.5 * total * shrink
        energy = parts[chunk][:comps, :].astype(F32)
        forcing = jnp.maximum(cosine * along + sine * across, 0.0)
        result = energy * (base + forcing) + (0.2 * shrink) * work[...].astype(F32)
        result = jnp.where(frozen, energy, result).astype(BF16)
        result = jnp.dot(result, matrix, preferred_element_type=F32).astype(BF16)
        for k, row in enumerate(rows):
            out_ref[row] = result[:, k * width : (k + 1) * width]


def finish(
    kernels, first, groups, strides, bounds, coef, maps, places, totals, paired, held, parts, marks
):
    comps = kernels[0].shape[0]
    rows, width = maps[0].shape
    operands = [coef, *maps, *kernels, *places, *totals, *paired, *held, *parts]
    return pl.pallas_call(
        functools.partial(finish_body, len(kernels), first, groups, strides),
        out_shape=jax.ShapeDtypeStruct((rows, comps, width), BF16),
        in_specs=[SMEM] + [VMEM] * len(operands) + [ANY] * len(marks),
        out_specs=VMEM,
        scratch_shapes=[pltpu.VMEM(value.shape, BF16) for value in held],
        compiler_params=params(20),
        cost_estimate=product_cost(kernels, paired),
    )(bounds, *operands, *marks)


def next_plane(value):
    return lax.ppermute(value, "plane", [(i, (i + 1) % PLANES) for i in range(PLANES)])


def boundaries(top, bottom):
    places = lax.axis_size("place")
    geo, count = ("plane", "place"), PLANES * places
    if places != 2:
        return (
            lax.ppermute(bottom, geo, [(i, i + 1) for i in range(count - 1)]),
            lax.ppermute(top, geo, [(i + 1, i) for i in range(count - 1)]),
        )
    first = lax.axis_index("place") == 0
    inside = lax.ppermute(jnp.where(first, bottom, top), "place", [(0, 1), (1, 0)])
    pairs = [(i, i + 1) for i in range(1, count - 1, 2)]
    outside = lax.ppermute(jnp.where(first, top, bottom), geo, pairs + [(j, i) for i, j in pairs])
    return inside, outside


def before_and_after(inside, outside):
    if lax.axis_size("place") != 2:
        return inside, outside
    first = lax.axis_index("place") == 0
    return jnp.where(first, outside, inside), jnp.where(first, inside, outside)


def with_partners(kernel):
    count = lax.axis_size("place")
    found = [kernel]
    for shift in range(1, count):
        pairs = [(i, (i + shift) % count) for i in range(count)]
        found.append(lax.ppermute(kernel, "place", pairs))
    return found


def ranks_of(owner_map):
    count = lax.axis_size("place")
    plane, place = lax.axis_index("plane"), lax.axis_index("place")
    steps = lax.rem(plane + PLANES - owner_map // count, PLANES)
    shift = lax.rem(place + count - lax.rem(owner_map, count), count)
    return steps * count + shift


def send_spec(value, flip):
    return lax.ppermute(value, "spec", [(i, i ^ flip) for i in range(4)])


def per_device(
    spectrum,
    sea_map,
    depth_factor,
    wind_speed,
    wind_dir,
    ice_mask,
    owner_map,
    pair_kernel,
    transfer_kernel,
):
    comps, rows, width = spectrum.shape
    here = lax.axis_index("spec")

    own_rows = lax.dynamic_slice_in_dim(transfer_kernel[0], here * comps, comps, axis=0)
    one_back = next_plane(own_rows)
    sea = sea_map.astype(F32)
    top = spectrum[:, 0] * sea_map[0].astype(BF16)
    bottom = spectrum[:, rows - 1] * sea_map[rows - 1].astype(BF16)
    halos = boundaries(top, bottom)
    x = spectrum.transpose(1, 0, 2)

    component = here * comps + jnp.arange(comps, dtype=jnp.int32)
    frequency = (component // NDIR).astype(F32)
    heading = 2.0 * math.pi * ((component % NDIR).astype(F32) + 0.5) / NDIR
    cosine, sine = jnp.cos(heading), jnp.sin(heading)
    gain = jnp.float32(1.1) ** (-0.5 * frequency)
    coef = jnp.stack(
        [
            0.7 * gain * jnp.abs(cosine),
            0.7 * gain * jnp.abs(sine),
            (cosine > 0).astype(F32),
            (sine > 0).astype(F32),
            cosine,
            sine,
        ],
        axis=1,
    )

    here_ref = jnp.reshape(here, (1,)).astype(jnp.int32)
    wide = 3 * rows // 8
    one, two = 1 + wide, 1 + 2 * wide
    groups = [list(range(1, one)), list(range(one, two)), [0] + list(range(two, rows))]

    def meet(part):
        return [send_spec(part, 1), send_spec(part, 2)]

    count = lax.axis_size("place")
    owners = PLANES * count
    rank_map = ranks_of(owner_map)
    kinds = jnp.arange(owners + 1, dtype=jnp.int32)
    bounds = []
    for group in groups:
        ranks = jnp.concatenate([rank_map[row] for row in group])
        bounds.append(jnp.sum((ranks[None, :] < kinds[:, None]).astype(jnp.int32), axis=1))
    bounds = jnp.concatenate(bounds)
    strides = [i * (owners + 1) for i in range(len(groups))]

    def move_rows(group, west, east):
        return propagate(
            group, owners, x, west, east, sea, depth_factor, coef, rank_map
        )

    none = jnp.zeros_like(top)
    parts, places = zip(*(move_rows(group, none, none) for group in groups[:2]))
    parts, places = list(parts), list(places)
    near = [meet(parts[0])]
    one_back, halos, near[0], sent = lax.optimization_barrier(
        (one_back, halos, near[0], parts[1])
    )

    two_back = next_plane(one_back)
    near.append(meet(sent))
    crossed = [send_spec(near[0][1], 1), send_spec(near[1][0], 2)]
    part, place = move_rows(groups[2], *before_and_after(*halos))
    parts.append(part)
    places.append(place)
    found = with_partners(own_rows) + with_partners(one_back)
    marks = [value[:8, :128] for value in (found[1], found[count + 1])]
    two_back, crossed, near[1], sent, marks = lax.optimization_barrier(
        (two_back, crossed, near[1], parts[2], marks)
    )
    near.append(meet(sent))
    three_back = next_plane(two_back)
    later = with_partners(two_back)
    paired, totals = [], []

    def pair_group(i, far):
        more, total = pair_up(here_ref, [[parts[i], *near[i], far]], pair_kernel)
        paired.extend(more)
        return total[0]

    totals.append(pair_group(0, crossed[0]))
    near[2], totals[0] = lax.optimization_barrier((near[2], totals[0]))
    last_cross = send_spec(near[2][1], 1)
    totals.append(pair_group(1, crossed[1]))
    some = found + later
    held, mark = transfer_all(some, 0, strides[:2], bounds, paired, [None] * 2)
    last_cross, mark = lax.optimization_barrier((last_cross, mark))
    total = pair_group(2, last_cross)
    three_back, total = lax.optimization_barrier((three_back, total))
    totals.append(total)
    last = with_partners(three_back)
    more, other = transfer_all(some, 0, strides[2:], bounds, paired[2:], [None])
    held += more
    if last[:-2]:
        held, _ = transfer_all(last[:-2], 3 * count, strides, bounds, paired, held)
    last = last[-2:]
    maps = [ice_mask, wind_speed, wind_dir]
    out = finish(
        last,
        owners - len(last),
        groups,
        strides,
        bounds,
        coef,
        maps,
        places,
        totals,
        paired,
        held,
        parts,
        [mark, other, *marks],
    )
    return out.transpose(1, 0, 2)


def solution(mesh):
    spec, geo = mesh.shape["spec"], mesh.shape["geo"]
    split = Mesh(
        mesh.devices.reshape(spec, PLANES, geo // PLANES), ("spec", "plane", "place")
    )
    tiles = ("plane", "place")
    placed = (
        P("spec", tiles, None),
        P(tiles, None),
        P(tiles, None),
        P(tiles, None),
        P(tiles, None),
        P(tiles, None),
        P(tiles, None),
        P(),
        P(tiles, None, None),
    )
    return jax.shard_map(
        per_device, mesh=split, in_specs=placed, out_specs=P("spec", tiles, None), check_vma=False
    )
```

```python
import functools
import math

import jax
import jax.numpy as jnp
from jax import lax
from jax.experimental import pallas as pl
from jax.experimental.pallas import tpu as pltpu
from jax.sharding import Mesh
from jax.sharding import PartitionSpec as P

NDIR = 36
PLANES = 4
SUB = 16
ANY = pl.BlockSpec(memory_space=pl.ANY)
VMEM = pl.BlockSpec(memory_space=pltpu.VMEM)
SMEM = pl.BlockSpec(memory_space=pltpu.SMEM)
BF16 = jnp.bfloat16
F32 = jnp.float32


def params(mib):
    return pltpu.CompilerParams(vmem_limit_bytes=mib * 2**20)


def places_of(rank, count):
    cells = rank.shape[1]
    kind = lax.broadcasted_iota(jnp.int32, (count, cells), 0)
    mine = (kind == rank).astype(F32)
    first = lax.broadcasted_iota(jnp.int32, (cells, cells), 0)
    second = lax.broadcasted_iota(jnp.int32, (cells, cells), 1)
    earlier = (first < second).astype(F32).astype(BF16)
    before = jnp.dot(mine.astype(BF16), earlier, preferred_element_type=F32)
    number = jnp.sum(mine, axis=1, keepdims=True)
    lower = (kind < rank).astype(F32)
    return jnp.sum(mine * before + lower * number, axis=0, keepdims=True)


def moves(place):
    cells = place.shape[1]
    target = lax.broadcasted_iota(jnp.int32, (cells, cells), 0)
    return (target == place.astype(jnp.int32)).astype(F32).astype(BF16)


def put_in_order(values, matrix):
    return lax.dot_general(
        values, matrix, (((1,), (1,)), ((), ())), preferred_element_type=F32
    )


def cells_of(values, rows):
    return jnp.concatenate([values[row : row + 1, :] for row in rows], axis=1)


def propagate_kernel(
    wanted,
    count,
    x_ref,
    west_ref,
    east_ref,
    sea_ref,
    depth_ref,
    coef_ref,
    rank_ref,
    sorted_ref,
    place_ref,
    out_ref,
):
    rows, comps, width = x_ref.shape

    def tile(at, height):
        lane = lax.broadcasted_iota(jnp.int32, (height, width), 1)
        coef = coef_ref[at, :]
        gain_x, gain_y, pos_x, pos_y = (
            jnp.broadcast_to(coef[:, i : i + 1], (height, width)) for i in range(4)
        )
        from_west, from_south = pos_x > 0, pos_y > 0
        first, last = lane == 0, lane == width - 1
        known = {}

        def masked(row):
            if row not in known:
                if row < 0:
                    known[row] = west_ref[at, :].astype(F32)
                elif row == rows:
                    known[row] = east_ref[at, :].astype(F32)
                else:
                    known[row] = x_ref[row, at, :].astype(F32) * sea_ref[row : row + 1, :]
            return known[row]

        for k, row in enumerate(wanted):
            west, centre, east = masked(row - 1), masked(row), masked(row + 1)
            upwind_x = jnp.where(from_west, west, east)
            south = jnp.where(first, 0.0, pltpu.roll(centre, 1, 1))
            north = jnp.where(last, 0.0, pltpu.roll(centre, width - 1, 1))
            upwind_y = jnp.where(from_south, south, north)
            depth = depth_ref[row : row + 1, :]
            moved = (
                centre
                - gain_x * depth * (centre - upwind_x)
                - gain_y * depth * (centre - upwind_y)
            )
            out_ref[at, k * width : (k + 1) * width] = (
                moved * sea_ref[row : row + 1, :]
            ).astype(BF16)

    def body(step, carry):
        tile(pl.ds(pl.multiple_of(step * SUB, SUB), SUB), SUB)
        return carry

    whole = comps // SUB
    lax.fori_loop(0, whole, body, 0)
    if comps % SUB:
        spare = out_ref.shape[0] - whole * SUB
        out_ref[whole * SUB :, :] = jnp.zeros((spare, out_ref.shape[1]), BF16)
        tile(slice(whole * SUB, comps), comps - whole * SUB)
    place = places_of(cells_of(rank_ref, wanted), count)
    place_ref[...] = place
    sorted_ref[...] = put_in_order(out_ref[...], moves(place)).astype(BF16)


def propagate(wanted, count, x, west, east, sea, depth, coef, rank_map):
    comps, width = x.shape[1:]
    padded = -(-comps // SUB) * SUB
    cells = len(wanted) * width
    return pl.pallas_call(
        functools.partial(propagate_kernel, wanted, count),
        out_shape=[
            jax.ShapeDtypeStruct((padded, cells), BF16),
            jax.ShapeDtypeStruct((1, cells), F32),
        ],
        in_specs=[VMEM] * 7,
        out_specs=[VMEM] * 2,
        scratch_shapes=[pltpu.VMEM((padded, cells), BF16)],
        compiler_params=params(20),
        cost_estimate=pl.CostEstimate(
            flops=2 * comps * cells, bytes_accessed=comps * cells, transcendentals=0
        ),
    )(x, west, east, sea, depth, coef, rank_map)


def split(refs, *sizes):
    out, at = [], 0
    for size in sizes:
        out.append(refs[at : at + size])
        at += size
    return out


def pair_body(tile, sizes, here_ref, *refs):
    groups = len(sizes)
    *parts, (pair_ref,), paired, totals, wholes = split(refs, *sizes, 1, groups, groups, groups)
    step = pl.program_id(0)
    comps = wholes[0].shape[0]
    some = comps // 4

    @pl.when(step == 0)
    def _():
        for here in range(4):

            @pl.when(here_ref[0] == here)
            def _(here=here):
                for pieces, whole in zip(parts, wholes):
                    for flip, piece in enumerate(pieces):
                        at = (here ^ flip) * some
                        whole[at : at + some, :] = piece[:some, :]

        for total, whole in zip(totals, wholes):
            total[...] = jnp.sum(whole[...].astype(F32), axis=0, keepdims=True) / comps

    for out_ref, whole in zip(paired, wholes):
        coupled = jnp.dot(pair_ref[...], whole[...], preferred_element_type=F32)
        own = whole[pl.ds(pl.multiple_of(step * tile, SUB), tile), :]
        out_ref[...] = (own.astype(F32) * coupled).astype(BF16)


def pair_up(here, groups, pair, tile=432):
    comps = pair.shape[0]
    sizes = [len(group) for group in groups]
    cells = [group[0].shape[1] for group in groups]
    flat = sum(groups, [])
    specs = [
        pl.BlockSpec(part.shape, lambda i: (0, 0), pipeline_mode=pl.Buffered(1)) for part in flat
    ]
    out = pl.pallas_call(
        functools.partial(pair_body, tile, sizes),
        grid=(comps // tile,),
        out_shape=[jax.ShapeDtypeStruct((comps, n), BF16) for n in cells]
        + [jax.ShapeDtypeStruct((1, n), F32) for n in cells],
        in_specs=[SMEM] + specs + [pl.BlockSpec((tile, comps), lambda i: (i, 0))],
        out_specs=[pl.BlockSpec((tile, n), lambda i: (i, 0)) for n in cells]
        + [pl.BlockSpec((1, n), lambda i: (0, 0)) for n in cells],
        scratch_shapes=[pltpu.VMEM((comps, n), BF16) for n in cells],
        compiler_params=params(20),
        cost_estimate=pl.CostEstimate(
            flops=comps * comps * sum(cells) // 4,
            bytes_accessed=comps * comps // 4,
            transcendentals=0,
        ),
    )(here, *flat, pair)
    return list(out[: len(groups)]), list(out[len(groups) :])


def apply_ranks(bounds_ref, at, which, paired, kernels, out, wide=256):
    cells = out.shape[1]
    for rank, kernel in which:
        begin, end = bounds_ref[at + rank], bounds_ref[at + rank + 1]
        for column in range(0, cells, wide):
            here = slice(column, column + wide)

            @pl.when((begin < column + wide) & (end > column))
            def _(here=here, column=column, kernel=kernel, begin=begin, end=end):
                term = jnp.dot(kernels[kernel][...], paired[:, here], preferred_element_type=F32)
                number = column + lax.broadcasted_iota(jnp.int32, term.shape, 1)
                mine = (number >= begin) & (number < end)
                out[:, here] = jnp.where(mine, term, out[:, here].astype(F32)).astype(BF16)


def product_cost(kernels, paired):
    flops = len(kernels) * kernels[0].size * sum(p.shape[1] for p in paired)
    moved = 2 * (len(kernels) * kernels[0].size + sum(p.size for p in paired))
    return pl.CostEstimate(flops=flops // 8, bytes_accessed=moved // 8, transcendentals=0)


def transfer_body(uses, strides, kept, bounds_ref, *refs):
    count, chunks = 1 + max(k for use in uses for _, k in use), len(uses)
    kernels, paired, held, outs, (mark,) = split(refs, count, chunks, len(kept), chunks, 1)
    mark[...] = jnp.zeros(mark.shape, F32)
    for chunk, out_ref in enumerate(outs):
        if chunk in kept:
            out_ref[...] = held[kept.index(chunk)][...]
        else:
            out_ref[...] = jnp.zeros(out_ref.shape, BF16)
        apply_ranks(bounds_ref, strides[chunk], uses[chunk], paired[chunk], kernels, out_ref)


def transfer(kernels, uses, strides, bounds, paired, held):
    kept = [i for i, value in enumerate(held) if value is not None]
    operands = [*kernels, *paired, *(held[i] for i in kept)]
    shapes = [jax.ShapeDtypeStruct((kernels[0].shape[0], p.shape[1]), BF16) for p in paired]
    shapes.append(jax.ShapeDtypeStruct((8, 128), F32))
    *held, mark = pl.pallas_call(
        functools.partial(transfer_body, uses, strides, kept),
        out_shape=shapes,
        in_specs=[SMEM] + [VMEM] * len(operands),
        out_specs=[VMEM] * len(shapes),
        compiler_params=params(8),
        cost_estimate=product_cost(kernels, paired),
    )(bounds, *operands)
    return held, mark


def transfer_all(kernels, first, strides, bounds, paired, held, most=6):
    mark = None
    for at in range(0, len(kernels), most):
        some = kernels[at : at + most]
        use = [(first + at + k, k) for k in range(len(some))]
        held, mark = transfer(some, [use] * len(paired), strides, bounds, paired, held)
    return held, mark


def finish_body(
    count, first, groups, strides, bounds_ref, coef_ref, ice_ref, speed_ref, angle_ref, *refs
):
    chunks = len(groups)
    kernels, places, totals, paired, held, parts = split(
        refs, count, chunks, chunks, chunks, chunks, chunks
    )
    out_ref, *works = refs[len(refs) - 1 - chunks :]
    comps, width = out_ref.shape[1:]
    maps = [speed_ref[...].astype(F32), angle_ref[...].astype(F32), ice_ref[...].astype(F32)]
    cosine, sine = coef_ref[:, 4:5], coef_ref[:, 5:6]
    for chunk, rows in enumerate(groups):
        work = works[chunk]
        work[...] = held[chunk][...]
        which = [(first + k, k) for k in range(count)]
        apply_ranks(bounds_ref, strides[chunk], which, paired[chunk], kernels, work)
        matrix = moves(places[chunk][...])
        given = [cells_of(values, rows) for values in maps]
        given = jnp.concatenate(given + [jnp.zeros_like(given[0])] * 5, axis=0)
        given = put_in_order(given.astype(BF16), matrix)
        speed, angle, frozen = 0.3 * given[0:1], given[1:2], given[2:3] > 0.5
        along, across = speed * jnp.cos(angle), speed * jnp.sin(angle)
        total = totals[chunk][...]
        shrink = 1.0 / (1.0 + total)
        base = 1.0 - 0.5 * total * shrink
        energy = parts[chunk][:comps, :].astype(F32)
        forcing = jnp.maximum(cosine * along + sine * across, 0.0)
        result = energy * (base + forcing) + (0.2 * shrink) * work[...].astype(F32)
        result = jnp.where(frozen, energy, result).astype(BF16)
        result = jnp.dot(result, matrix, preferred_element_type=F32).astype(BF16)
        for k, row in enumerate(rows):
            out_ref[row] = result[:, k * width : (k + 1) * width]


def finish(
    kernels, first, groups, strides, bounds, coef, maps, places, totals, paired, held, parts, marks
):
    comps = kernels[0].shape[0]
    rows, width = maps[0].shape
    operands = [coef, *maps, *kernels, *places, *totals, *paired, *held, *parts]
    return pl.pallas_call(
        functools.partial(finish_body, len(kernels), first, groups, strides),
        out_shape=jax.ShapeDtypeStruct((rows, comps, width), BF16),
        in_specs=[SMEM] + [VMEM] * len(operands) + [ANY] * len(marks),
        out_specs=VMEM,
        scratch_shapes=[pltpu.VMEM(value.shape, BF16) for value in held],
        compiler_params=params(20),
        cost_estimate=product_cost(kernels, paired),
    )(bounds, *operands, *marks)


def next_plane(value):
    return lax.ppermute(value, "plane", [(i, (i + 1) % PLANES) for i in range(PLANES)])


def boundaries(top, bottom):
    places = lax.axis_size("place")
    geo, count = ("plane", "place"), PLANES * places
    if places != 2:
        return (
            lax.ppermute(bottom, geo, [(i, i + 1) for i in range(count - 1)]),
            lax.ppermute(top, geo, [(i + 1, i) for i in range(count - 1)]),
        )
    first = lax.axis_index("place") == 0
    inside = lax.ppermute(jnp.where(first, bottom, top), "place", [(0, 1), (1, 0)])
    pairs = [(i, i + 1) for i in range(1, count - 1, 2)]
    outside = lax.ppermute(jnp.where(first, top, bottom), geo, pairs + [(j, i) for i, j in pairs])
    return inside, outside


def before_and_after(inside, outside):
    if lax.axis_size("place") != 2:
        return inside, outside
    first = lax.axis_index("place") == 0
    return jnp.where(first, outside, inside), jnp.where(first, inside, outside)


def with_partners(kernel):
    count = lax.axis_size("place")
    found = [kernel]
    for shift in range(1, count):
        pairs = [(i, (i + shift) % count) for i in range(count)]
        found.append(lax.ppermute(kernel, "place", pairs))
    return found


def ranks_of(owner_map):
    count = lax.axis_size("place")
    plane, place = lax.axis_index("plane"), lax.axis_index("place")
    steps = lax.rem(plane + PLANES - owner_map // count, PLANES)
    shift = lax.rem(place + count - lax.rem(owner_map, count), count)
    return steps * count + shift


def send_spec(value, flip):
    return lax.ppermute(value, "spec", [(i, i ^ flip) for i in range(4)])


def per_device(
    spectrum,
    sea_map,
    depth_factor,
    wind_speed,
    wind_dir,
    ice_mask,
    owner_map,
    pair_kernel,
    transfer_kernel,
):
    comps, rows, width = spectrum.shape
    here = lax.axis_index("spec")

    own_rows = lax.dynamic_slice_in_dim(transfer_kernel[0], here * comps, comps, axis=0)
    one_back = next_plane(own_rows)
    sea = sea_map.astype(F32)
    top = spectrum[:, 0] * sea_map[0].astype(BF16)
    bottom = spectrum[:, rows - 1] * sea_map[rows - 1].astype(BF16)
    halos = boundaries(top, bottom)
    x = spectrum.transpose(1, 0, 2)

    component = here * comps + jnp.arange(comps, dtype=jnp.int32)
    frequency = (component // NDIR).astype(F32)
    heading = 2.0 * math.pi * ((component % NDIR).astype(F32) + 0.5) / NDIR
    cosine, sine = jnp.cos(heading), jnp.sin(heading)
    gain = jnp.float32(1.1) ** (-0.5 * frequency)
    coef = jnp.stack(
        [
            0.7 * gain * jnp.abs(cosine),
            0.7 * gain * jnp.abs(sine),
            (cosine > 0).astype(F32),
            (sine > 0).astype(F32),
            cosine,
            sine,
        ],
        axis=1,
    )

    here_ref = jnp.reshape(here, (1,)).astype(jnp.int32)
    wide = 3 * rows // 8
    one, two = 1 + wide, 1 + 2 * wide
    groups = [list(range(1, one)), list(range(one, two)), [0] + list(range(two, rows))]

    def meet(part):
        return [send_spec(part, 1), send_spec(part, 2)]

    count = lax.axis_size("place")
    owners = PLANES * count
    rank_map = ranks_of(owner_map)
    kinds = jnp.arange(owners + 1, dtype=jnp.int32)
    bounds = []
    for group in groups:
        ranks = jnp.concatenate([rank_map[row] for row in group])
        bounds.append(jnp.sum((ranks[None, :] < kinds[:, None]).astype(jnp.int32), axis=1))
    bounds = jnp.concatenate(bounds)
    strides = [i * (owners + 1) for i in range(len(groups))]

    def move_rows(group, west, east):
        return propagate(
            group, owners, x, west, east, sea, depth_factor, coef, rank_map
        )

    none = jnp.zeros_like(top)
    parts, places = zip(*(move_rows(group, none, none) for group in groups[:2]))
    parts, places = list(parts), list(places)
    near = [meet(parts[0])]
    one_back, halos, near[0], sent, own_now = lax.optimization_barrier(
        (one_back, halos, near[0], parts[1], own_rows)
    )

    def pair_group(i, far):
        (more,), (total,) = pair_up(here_ref, [[parts[i], *near[i], far]], pair_kernel)
        paired.append(more)
        totals.append(total)

    paired, totals = [], []
    two_back = next_plane(one_back)
    crossed = send_spec(near[0][1], 1)
    other = send_spec(sent, 2)
    part, place = move_rows(groups[2], *before_and_after(*halos))
    crossed, sent, place = lax.optimization_barrier((crossed, sent, place))
    near.append([send_spec(sent, 1), other])
    parts.append(part)
    places.append(place)
    second = send_spec(part, 2)
    found = with_partners(own_now) + with_partners(one_back)
    marks = [value[:8, :128] for value in (found[1], found[count + 1])]
    pair_group(0, crossed)
    two_back, near[1], second, sent, totals, marks = lax.optimization_barrier(
        (two_back, near[1], second, part, totals, marks)
    )

    three_back = next_plane(two_back)
    later = with_partners(two_back)
    crossed = send_spec(near[1][0], 2)
    near.append([send_spec(sent, 1), second])
    last_cross = send_spec(second, 1)
    some = found + later
    held, mark = transfer_all(some, 0, strides[:1], bounds, paired, [None])
    crossed, mark = lax.optimization_barrier((crossed, mark))
    marks.append(mark)
    pair_group(1, crossed)
    last_cross, totals[1] = lax.optimization_barrier((last_cross, totals[1]))
    pair_group(2, last_cross)
    more, mark = transfer_all(some, 0, strides[1:2], bounds, paired[1:2], [None])
    held += more
    three_back, mark, totals[2] = lax.optimization_barrier((three_back, mark, totals[2]))
    marks.append(mark)
    last = with_partners(three_back)
    more, mark = transfer_all(some, 0, strides[2:], bounds, paired[2:], [None])
    held += more
    marks.append(mark)
    if last[:-2]:
        held, _ = transfer_all(last[:-2], 3 * count, strides, bounds, paired, held)
    last = last[-2:]
    maps = [ice_mask, wind_speed, wind_dir]
    out = finish(
        last,
        owners - len(last),
        groups,
        strides,
        bounds,
        coef,
        maps,
        places,
        totals,
        paired,
        held,
        parts,
        marks,
    )
    return out.transpose(1, 0, 2)


def solution(mesh):
    spec, geo = mesh.shape["spec"], mesh.shape["geo"]
    split = Mesh(
        mesh.devices.reshape(spec, PLANES, geo // PLANES), ("spec", "plane", "place")
    )
    tiles = ("plane", "place")
    placed = (
        P("spec", tiles, None),
        P(tiles, None),
        P(tiles, None),
        P(tiles, None),
        P(tiles, None),
        P(tiles, None),
        P(tiles, None),
        P(),
        P(tiles, None, None),
    )
    return jax.shard_map(
        per_device, mesh=split, in_specs=placed, out_specs=P("spec", tiles, None), check_vma=False
    )
```

```python
import functools
import math

import jax
import jax.numpy as jnp
from jax import lax
from jax.experimental import pallas as pl
from jax.experimental.pallas import tpu as pltpu
from jax.sharding import Mesh
from jax.sharding import PartitionSpec as P

NDIR = 36
PLANES = 4
SUB = 16
ANY = pl.BlockSpec(memory_space=pl.ANY)
VMEM = pl.BlockSpec(memory_space=pltpu.VMEM)
SMEM = pl.BlockSpec(memory_space=pltpu.SMEM)
BF16 = jnp.bfloat16
F32 = jnp.float32


def params(mib):
    return pltpu.CompilerParams(vmem_limit_bytes=mib * 2**20)


def places_of(rank, count):
    cells = rank.shape[1]
    kind = lax.broadcasted_iota(jnp.int32, (count, cells), 0)
    mine = (kind == rank).astype(F32)
    first = lax.broadcasted_iota(jnp.int32, (cells, cells), 0)
    second = lax.broadcasted_iota(jnp.int32, (cells, cells), 1)
    earlier = (first < second).astype(F32).astype(BF16)
    before = jnp.dot(mine.astype(BF16), earlier, preferred_element_type=F32)
    number = jnp.sum(mine, axis=1, keepdims=True)
    lower = (kind < rank).astype(F32)
    return jnp.sum(mine * before + lower * number, axis=0, keepdims=True)


def moves(place):
    cells = place.shape[1]
    target = lax.broadcasted_iota(jnp.int32, (cells, cells), 0)
    return (target == place.astype(jnp.int32)).astype(F32).astype(BF16)


def put_in_order(values, matrix):
    return lax.dot_general(
        values, matrix, (((1,), (1,)), ((), ())), preferred_element_type=F32
    )


def cells_of(values, rows):
    return jnp.concatenate([values[row : row + 1, :] for row in rows], axis=1)


def propagate_kernel(
    wanted,
    count,
    x_ref,
    west_ref,
    east_ref,
    sea_ref,
    depth_ref,
    coef_ref,
    rank_ref,
    sorted_ref,
    place_ref,
    out_ref,
):
    rows, comps, width = x_ref.shape

    def tile(at, height):
        lane = lax.broadcasted_iota(jnp.int32, (height, width), 1)
        coef = coef_ref[at, :]
        gain_x, gain_y, pos_x, pos_y = (
            jnp.broadcast_to(coef[:, i : i + 1], (height, width)) for i in range(4)
        )
        from_west, from_south = pos_x > 0, pos_y > 0
        first, last = lane == 0, lane == width - 1
        known = {}

        def masked(row):
            if row not in known:
                if row < 0:
                    known[row] = west_ref[at, :].astype(F32)
                elif row == rows:
                    known[row] = east_ref[at, :].astype(F32)
                else:
                    known[row] = x_ref[row, at, :].astype(F32) * sea_ref[row : row + 1, :]
            return known[row]

        for k, row in enumerate(wanted):
            west, centre, east = masked(row - 1), masked(row), masked(row + 1)
            upwind_x = jnp.where(from_west, west, east)
            south = jnp.where(first, 0.0, pltpu.roll(centre, 1, 1))
            north = jnp.where(last, 0.0, pltpu.roll(centre, width - 1, 1))
            upwind_y = jnp.where(from_south, south, north)
            depth = depth_ref[row : row + 1, :]
            moved = (
                centre
                - gain_x * depth * (centre - upwind_x)
                - gain_y * depth * (centre - upwind_y)
            )
            out_ref[at, k * width : (k + 1) * width] = (
                moved * sea_ref[row : row + 1, :]
            ).astype(BF16)

    def body(step, carry):
        tile(pl.ds(pl.multiple_of(step * SUB, SUB), SUB), SUB)
        return carry

    whole = comps // SUB
    lax.fori_loop(0, whole, body, 0)
    if comps % SUB:
        spare = out_ref.shape[0] - whole * SUB
        out_ref[whole * SUB :, :] = jnp.zeros((spare, out_ref.shape[1]), BF16)
        tile(slice(whole * SUB, comps), comps - whole * SUB)
    place = places_of(cells_of(rank_ref, wanted), count)
    place_ref[...] = place
    sorted_ref[...] = put_in_order(out_ref[...], moves(place))[:comps].astype(BF16)


def propagate(wanted, count, x, west, east, sea, depth, coef, rank_map):
    comps, width = x.shape[1:]
    padded = -(-comps // SUB) * SUB
    cells = len(wanted) * width
    return pl.pallas_call(
        functools.partial(propagate_kernel, wanted, count),
        out_shape=[
            jax.ShapeDtypeStruct((comps, cells), BF16),
            jax.ShapeDtypeStruct((1, cells), F32),
        ],
        in_specs=[VMEM] * 7,
        out_specs=[VMEM] * 2,
        scratch_shapes=[pltpu.VMEM((padded, cells), BF16)],
        compiler_params=params(20),
        cost_estimate=pl.CostEstimate(
            flops=2 * comps * cells, bytes_accessed=comps * cells, transcendentals=0
        ),
    )(x, west, east, sea, depth, coef, rank_map)


def split(refs, *sizes):
    out, at = [], 0
    for size in sizes:
        out.append(refs[at : at + size])
        at += size
    return out


def pair_body(tile, sizes, here_ref, *refs):
    groups = len(sizes)
    *parts, (pair_ref,), paired, totals, wholes = split(refs, *sizes, 1, groups, groups, groups)
    step = pl.program_id(0)
    comps = wholes[0].shape[0]
    some = comps // 4

    @pl.when(step == 0)
    def _():
        for here in range(4):

            @pl.when(here_ref[0] == here)
            def _(here=here):
                for pieces, whole in zip(parts, wholes):
                    for flip, piece in enumerate(pieces):
                        at = (here ^ flip) * some
                        whole[at : at + some, :] = piece[:some, :]

        for total, whole in zip(totals, wholes):
            total[...] = jnp.sum(whole[...].astype(F32), axis=0, keepdims=True) / comps

    for out_ref, whole in zip(paired, wholes):
        coupled = jnp.dot(pair_ref[...], whole[...], preferred_element_type=F32)
        own = whole[pl.ds(pl.multiple_of(step * tile, SUB), tile), :]
        out_ref[...] = (own.astype(F32) * coupled).astype(BF16)


def pair_up(here, groups, pair, tile=432):
    comps = pair.shape[0]
    sizes = [len(group) for group in groups]
    cells = [group[0].shape[1] for group in groups]
    flat = sum(groups, [])
    specs = [
        pl.BlockSpec(part.shape, lambda i: (0, 0), pipeline_mode=pl.Buffered(1)) for part in flat
    ]
    out = pl.pallas_call(
        functools.partial(pair_body, tile, sizes),
        grid=(comps // tile,),
        out_shape=[jax.ShapeDtypeStruct((comps, n), BF16) for n in cells]
        + [jax.ShapeDtypeStruct((1, n), F32) for n in cells],
        in_specs=[SMEM] + specs + [pl.BlockSpec((tile, comps), lambda i: (i, 0))],
        out_specs=[pl.BlockSpec((tile, n), lambda i: (i, 0)) for n in cells]
        + [pl.BlockSpec((1, n), lambda i: (0, 0)) for n in cells],
        scratch_shapes=[pltpu.VMEM((comps, n), BF16) for n in cells],
        compiler_params=params(20),
        cost_estimate=pl.CostEstimate(
            flops=comps * comps * sum(cells) // 4,
            bytes_accessed=comps * comps // 4,
            transcendentals=0,
        ),
    )(here, *flat, pair)
    return list(out[: len(groups)]), list(out[len(groups) :])


def apply_ranks(bounds_ref, at, which, paired, kernels, out, wide=256):
    cells = out.shape[1]
    for rank, kernel in which:
        begin, end = bounds_ref[at + rank], bounds_ref[at + rank + 1]
        for column in range(0, cells, wide):
            here = slice(column, column + wide)

            @pl.when((begin < column + wide) & (end > column))
            def _(here=here, column=column, kernel=kernel, begin=begin, end=end):
                term = jnp.dot(kernels[kernel][...], paired[:, here], preferred_element_type=F32)
                number = column + lax.broadcasted_iota(jnp.int32, term.shape, 1)
                mine = (number >= begin) & (number < end)
                out[:, here] = jnp.where(mine, term, out[:, here].astype(F32)).astype(BF16)


def product_cost(kernels, paired):
    flops = len(kernels) * kernels[0].size * sum(p.shape[1] for p in paired)
    moved = 2 * (len(kernels) * kernels[0].size + sum(p.size for p in paired))
    return pl.CostEstimate(flops=flops // 8, bytes_accessed=moved // 8, transcendentals=0)


def transfer_body(uses, strides, kept, bounds_ref, *refs):
    count, chunks = 1 + max(k for use in uses for _, k in use), len(uses)
    kernels, paired, held, outs, (mark,) = split(refs, count, chunks, len(kept), chunks, 1)
    mark[...] = jnp.zeros(mark.shape, F32)
    for chunk, out_ref in enumerate(outs):
        if chunk in kept:
            out_ref[...] = held[kept.index(chunk)][...]
        else:
            out_ref[...] = jnp.zeros(out_ref.shape, BF16)
        apply_ranks(bounds_ref, strides[chunk], uses[chunk], paired[chunk], kernels, out_ref)


def transfer(kernels, uses, strides, bounds, paired, held):
    kept = [i for i, value in enumerate(held) if value is not None]
    operands = [*kernels, *paired, *(held[i] for i in kept)]
    shapes = [jax.ShapeDtypeStruct((kernels[0].shape[0], p.shape[1]), BF16) for p in paired]
    shapes.append(jax.ShapeDtypeStruct((8, 128), F32))
    *held, mark = pl.pallas_call(
        functools.partial(transfer_body, uses, strides, kept),
        out_shape=shapes,
        in_specs=[SMEM] + [VMEM] * len(operands),
        out_specs=[VMEM] * len(shapes),
        compiler_params=params(8),
        cost_estimate=product_cost(kernels, paired),
    )(bounds, *operands)
    return held, mark


def transfer_all(kernels, first, strides, bounds, paired, held, most=6):
    mark = None
    for at in range(0, len(kernels), most):
        some = kernels[at : at + most]
        use = [(first + at + k, k) for k in range(len(some))]
        held, mark = transfer(some, [use] * len(paired), strides, bounds, paired, held)
    return held, mark


def wind_body(groups, ice_ref, speed_ref, angle_ref, *refs):
    places, outs = split(refs, len(groups), len(groups))
    maps = [speed_ref[...].astype(F32), angle_ref[...].astype(F32), ice_ref[...].astype(F32)]
    for rows, place, out_ref in zip(groups, places, outs):
        given = [cells_of(values, rows) for values in maps]
        given = jnp.concatenate(given + [jnp.zeros_like(given[0])] * 5, axis=0)
        given = put_in_order(given.astype(BF16), moves(place[...]))
        speed, angle, frozen = 0.3 * given[0:1], given[1:2], given[2:3]
        rest = [jnp.zeros_like(frozen)] * 5
        rows_out = [speed * jnp.cos(angle), speed * jnp.sin(angle), frozen] + rest
        out_ref[...] = jnp.concatenate(rows_out, axis=0)


def wind(groups, maps, places):
    return pl.pallas_call(
        functools.partial(wind_body, groups),
        out_shape=[jax.ShapeDtypeStruct((8, place.shape[1]), F32) for place in places],
        in_specs=[VMEM] * (len(maps) + len(places)),
        out_specs=[VMEM] * len(places),
        compiler_params=params(12),
        cost_estimate=pl.CostEstimate(flops=0, bytes_accessed=0, transcendentals=0),
    )(*maps, *places)


def finish_body(
    count, first, groups, strides, bounds_ref, coef_ref, *refs
):
    chunks = len(groups)
    kernels, places, winds, totals, paired, held, parts = split(
        refs, count, chunks, chunks, chunks, chunks, chunks, chunks
    )
    out_ref, *works = refs[len(refs) - 1 - chunks :]
    comps, width = out_ref.shape[1:]
    cosine, sine = coef_ref[:, 4:5], coef_ref[:, 5:6]
    for chunk, rows in enumerate(groups):
        work = works[chunk]
        work[...] = held[chunk][...]
        which = [(first + k, k) for k in range(count)]
        apply_ranks(bounds_ref, strides[chunk], which, paired[chunk], kernels, work)
        matrix = moves(places[chunk][...])
        along, across, frozen = (winds[chunk][i : i + 1, :] for i in range(3))
        total = totals[chunk][...]
        shrink = 1.0 / (1.0 + total)
        base = 1.0 - 0.5 * total * shrink
        energy = parts[chunk][:comps, :].astype(F32)
        forcing = jnp.maximum(cosine * along + sine * across, 0.0)
        result = energy * (base + forcing) + (0.2 * shrink) * work[...].astype(F32)
        result = jnp.where(frozen > 0.5, energy, result).astype(BF16)
        result = jnp.dot(result, matrix, preferred_element_type=F32).astype(BF16)
        for k, row in enumerate(rows):
            out_ref[row] = result[:, k * width : (k + 1) * width]


def finish(
    kernels, first, groups, width, strides, bounds, coef, places, winds, totals, paired, held, parts, marks
):
    comps = kernels[0].shape[0]
    rows = sum(place.shape[1] for place in places) // width
    operands = [coef, *kernels, *places, *winds, *totals, *paired, *held, *parts]
    return pl.pallas_call(
        functools.partial(finish_body, len(kernels), first, groups, strides),
        out_shape=jax.ShapeDtypeStruct((rows, comps, width), BF16),
        in_specs=[SMEM] + [VMEM] * len(operands) + [ANY] * len(marks),
        out_specs=VMEM,
        scratch_shapes=[pltpu.VMEM(value.shape, BF16) for value in held],
        compiler_params=params(20),
        cost_estimate=product_cost(kernels, paired),
    )(bounds, *operands, *marks)


def next_plane(value):
    return lax.ppermute(value, "plane", [(i, (i + 1) % PLANES) for i in range(PLANES)])


def boundaries(top, bottom):
    places = lax.axis_size("place")
    geo, count = ("plane", "place"), PLANES * places
    if places != 2:
        return (
            lax.ppermute(bottom, geo, [(i, i + 1) for i in range(count - 1)]),
            lax.ppermute(top, geo, [(i + 1, i) for i in range(count - 1)]),
        )
    first = lax.axis_index("place") == 0
    inside = lax.ppermute(jnp.where(first, bottom, top), "place", [(0, 1), (1, 0)])
    pairs = [(i, i + 1) for i in range(1, count - 1, 2)]
    outside = lax.ppermute(jnp.where(first, top, bottom), geo, pairs + [(j, i) for i, j in pairs])
    return inside, outside


def before_and_after(inside, outside):
    if lax.axis_size("place") != 2:
        return inside, outside
    first = lax.axis_index("place") == 0
    return jnp.where(first, outside, inside), jnp.where(first, inside, outside)


def with_partners(kernel):
    count = lax.axis_size("place")
    found = [kernel]
    for shift in range(1, count):
        pairs = [(i, (i + shift) % count) for i in range(count)]
        found.append(lax.ppermute(kernel, "place", pairs))
    return found


def ranks_of(owner_map):
    count = lax.axis_size("place")
    plane, place = lax.axis_index("plane"), lax.axis_index("place")
    steps = lax.rem(plane + PLANES - owner_map // count, PLANES)
    shift = lax.rem(place + count - lax.rem(owner_map, count), count)
    return steps * count + shift


def send_spec(value, flip):
    return lax.ppermute(value, "spec", [(i, i ^ flip) for i in range(4)])


def per_device(
    spectrum,
    sea_map,
    depth_factor,
    wind_speed,
    wind_dir,
    ice_mask,
    owner_map,
    pair_kernel,
    transfer_kernel,
):
    comps, rows, width = spectrum.shape
    here = lax.axis_index("spec")

    own_rows = lax.dynamic_slice_in_dim(transfer_kernel[0], here * comps, comps, axis=0)
    one_back = next_plane(own_rows)
    sea = sea_map.astype(F32)
    top = spectrum[:, 0] * sea_map[0].astype(BF16)
    bottom = spectrum[:, rows - 1] * sea_map[rows - 1].astype(BF16)
    halos = boundaries(top, bottom)
    x = spectrum.transpose(1, 0, 2)

    component = here * comps + jnp.arange(comps, dtype=jnp.int32)
    frequency = (component // NDIR).astype(F32)
    heading = 2.0 * math.pi * ((component % NDIR).astype(F32) + 0.5) / NDIR
    cosine, sine = jnp.cos(heading), jnp.sin(heading)
    gain = jnp.float32(1.1) ** (-0.5 * frequency)
    coef = jnp.stack(
        [
            0.7 * gain * jnp.abs(cosine),
            0.7 * gain * jnp.abs(sine),
            (cosine > 0).astype(F32),
            (sine > 0).astype(F32),
            cosine,
            sine,
        ],
        axis=1,
    )

    here_ref = jnp.reshape(here, (1,)).astype(jnp.int32)
    wide = 3 * rows // 8
    one, two = 1 + wide, 1 + 2 * wide
    groups = [list(range(1, one)), list(range(one, two)), [0] + list(range(two, rows))]

    def meet(part):
        return [send_spec(part, 1), send_spec(part, 2)]

    count = lax.axis_size("place")
    owners = PLANES * count
    rank_map = ranks_of(owner_map)
    kinds = jnp.arange(owners + 1, dtype=jnp.int32)
    bounds = []
    for group in groups:
        ranks = jnp.concatenate([rank_map[row] for row in group])
        bounds.append(jnp.sum((ranks[None, :] < kinds[:, None]).astype(jnp.int32), axis=1))
    bounds = jnp.concatenate(bounds)
    strides = [i * (owners + 1) for i in range(len(groups))]

    def move_rows(group, west, east):
        return propagate(
            group, owners, x, west, east, sea, depth_factor, coef, rank_map
        )

    none = jnp.zeros_like(top)
    parts, places = zip(*(move_rows(group, none, none) for group in groups[:2]))
    parts, places = list(parts), list(places)
    near = [meet(parts[0])]
    one_back, halos, near[0], sent, own_now = lax.optimization_barrier(
        (one_back, halos, near[0], parts[1], own_rows)
    )

    def pair_group(i, far):
        (more,), (total,) = pair_up(here_ref, [[parts[i], *near[i], far]], pair_kernel)
        paired.append(more)
        totals.append(total)

    paired, totals = [], []
    two_back = next_plane(one_back)
    crossed = send_spec(near[0][1], 1)
    other = send_spec(sent, 2)
    part, place = move_rows(groups[2], *before_and_after(*halos))
    crossed, sent, place = lax.optimization_barrier((crossed, sent, place))
    near.append([send_spec(sent, 1), other])
    parts.append(part)
    places.append(place)
    second = send_spec(part, 2)
    found = with_partners(own_now) + with_partners(one_back)
    marks = [value[:8, :128] for value in (found[1], found[count + 1])]
    pair_group(0, crossed)
    winds = wind(groups, [ice_mask, wind_speed, wind_dir], places)
    two_back, near[1], second, sent, totals, winds, marks = lax.optimization_barrier(
        (two_back, near[1], second, part, totals, winds, marks)
    )

    three_back = next_plane(two_back)
    later = with_partners(two_back)
    crossed = send_spec(near[1][0], 2)
    near.append([send_spec(sent, 1), second])
    last_cross = send_spec(second, 1)
    some = found + later
    held, mark = transfer_all(some, 0, strides[:1], bounds, paired, [None])
    crossed, mark = lax.optimization_barrier((crossed, mark))
    marks.append(mark)
    pair_group(1, crossed)
    last_cross, totals[1] = lax.optimization_barrier((last_cross, totals[1]))
    pair_group(2, last_cross)
    more, mark = transfer_all(some, 0, strides[1:2], bounds, paired[1:2], [None])
    held += more
    three_back, mark, totals[2] = lax.optimization_barrier((three_back, mark, totals[2]))
    marks.append(mark)
    last = with_partners(three_back)
    more, mark = transfer_all(some, 0, strides[2:], bounds, paired[2:], [None])
    held += more
    marks.append(mark)
    if last[:-2]:
        held, _ = transfer_all(last[:-2], 3 * count, strides, bounds, paired, held)
    last = last[-2:]
    out = finish(
        last,
        owners - len(last),
        groups,
        width,
        strides,
        bounds,
        coef,
        places,
        winds,
        totals,
        paired,
        held,
        parts,
        marks,
    )
    return out.transpose(1, 0, 2)


def solution(mesh):
    spec, geo = mesh.shape["spec"], mesh.shape["geo"]
    split = Mesh(
        mesh.devices.reshape(spec, PLANES, geo // PLANES), ("spec", "plane", "place")
    )
    tiles = ("plane", "place")
    placed = (
        P("spec", tiles, None),
        P(tiles, None),
        P(tiles, None),
        P(tiles, None),
        P(tiles, None),
        P(tiles, None),
        P(tiles, None),
        P(),
        P(tiles, None, None),
    )
    return jax.shard_map(
        per_device, mesh=split, in_specs=placed, out_specs=P("spec", tiles, None), check_vma=False
    )
```

```python
import functools
import math

import jax
import jax.numpy as jnp
from jax import lax
from jax.experimental import pallas as pl
from jax.experimental.pallas import tpu as pltpu
from jax.sharding import Mesh
from jax.sharding import PartitionSpec as P

NDIR = 36
PLANES = 4
SUB = 16
ANY = pl.BlockSpec(memory_space=pl.ANY)
VMEM = pl.BlockSpec(memory_space=pltpu.VMEM)
SMEM = pl.BlockSpec(memory_space=pltpu.SMEM)
BF16 = jnp.bfloat16
F32 = jnp.float32


def params(mib):
    return pltpu.CompilerParams(vmem_limit_bytes=mib * 2**20)


def places_of(rank, count):
    cells = rank.shape[1]
    kind = lax.broadcasted_iota(jnp.int32, (count, cells), 0)
    mine = (kind == rank).astype(F32)
    first = lax.broadcasted_iota(jnp.int32, (cells, cells), 0)
    second = lax.broadcasted_iota(jnp.int32, (cells, cells), 1)
    earlier = (first < second).astype(F32).astype(BF16)
    before = jnp.dot(mine.astype(BF16), earlier, preferred_element_type=F32)
    number = jnp.sum(mine, axis=1, keepdims=True)
    lower = (kind < rank).astype(F32)
    return jnp.sum(mine * before + lower * number, axis=0, keepdims=True)


def moves(place):
    cells = place.shape[1]
    target = lax.broadcasted_iota(jnp.int32, (cells, cells), 0)
    return (target == place.astype(jnp.int32)).astype(F32).astype(BF16)


def put_in_order(values, matrix):
    return lax.dot_general(
        values, matrix, (((1,), (1,)), ((), ())), preferred_element_type=F32
    )


def cells_of(values, rows):
    return jnp.concatenate([values[row : row + 1, :] for row in rows], axis=1)


def propagate_kernel(
    wanted,
    count,
    x_ref,
    west_ref,
    east_ref,
    sea_ref,
    depth_ref,
    coef_ref,
    rank_ref,
    sorted_ref,
    place_ref,
    out_ref,
):
    rows, comps, width = x_ref.shape

    def tile(at, height):
        lane = lax.broadcasted_iota(jnp.int32, (height, width), 1)
        coef = coef_ref[at, :]
        gain_x, gain_y, pos_x, pos_y = (
            jnp.broadcast_to(coef[:, i : i + 1], (height, width)) for i in range(4)
        )
        from_west, from_south = pos_x > 0, pos_y > 0
        first, last = lane == 0, lane == width - 1
        known = {}

        def masked(row):
            if row not in known:
                if row < 0:
                    known[row] = west_ref[at, :].astype(F32)
                elif row == rows:
                    known[row] = east_ref[at, :].astype(F32)
                else:
                    known[row] = x_ref[row, at, :].astype(F32) * sea_ref[row : row + 1, :]
            return known[row]

        for k, row in enumerate(wanted):
            west, centre, east = masked(row - 1), masked(row), masked(row + 1)
            upwind_x = jnp.where(from_west, west, east)
            south = jnp.where(first, 0.0, pltpu.roll(centre, 1, 1))
            north = jnp.where(last, 0.0, pltpu.roll(centre, width - 1, 1))
            upwind_y = jnp.where(from_south, south, north)
            depth = depth_ref[row : row + 1, :]
            moved = (
                centre
                - gain_x * depth * (centre - upwind_x)
                - gain_y * depth * (centre - upwind_y)
            )
            out_ref[at, k * width : (k + 1) * width] = (
                moved * sea_ref[row : row + 1, :]
            ).astype(BF16)

    def body(step, carry):
        tile(pl.ds(pl.multiple_of(step * SUB, SUB), SUB), SUB)
        return carry

    whole = comps // SUB
    lax.fori_loop(0, whole, body, 0)
    if comps % SUB:
        spare = out_ref.shape[0] - whole * SUB
        out_ref[whole * SUB :, :] = jnp.zeros((spare, out_ref.shape[1]), BF16)
        tile(slice(whole * SUB, comps), comps - whole * SUB)
    place = places_of(cells_of(rank_ref, wanted), count)
    place_ref[...] = place
    sorted_ref[...] = put_in_order(out_ref[...], moves(place))[:comps].astype(BF16)


def propagate(wanted, count, x, west, east, sea, depth, coef, rank_map):
    comps, width = x.shape[1:]
    padded = -(-comps // SUB) * SUB
    cells = len(wanted) * width
    return pl.pallas_call(
        functools.partial(propagate_kernel, wanted, count),
        out_shape=[
            jax.ShapeDtypeStruct((comps, cells), BF16),
            jax.ShapeDtypeStruct((1, cells), F32),
        ],
        in_specs=[VMEM] * 7,
        out_specs=[VMEM] * 2,
        scratch_shapes=[pltpu.VMEM((padded, cells), BF16)],
        compiler_params=params(20),
        cost_estimate=pl.CostEstimate(
            flops=2 * comps * cells, bytes_accessed=comps * cells, transcendentals=0
        ),
    )(x, west, east, sea, depth, coef, rank_map)


def split(refs, *sizes):
    out, at = [], 0
    for size in sizes:
        out.append(refs[at : at + size])
        at += size
    return out


def pair_body(tile, sizes, here_ref, *refs):
    groups = len(sizes)
    *parts, (pair_ref,), paired, totals, wholes = split(refs, *sizes, 1, groups, groups, groups)
    step = pl.program_id(0)
    comps = wholes[0].shape[0]
    some = comps // 4

    @pl.when(step == 0)
    def _():
        for here in range(4):

            @pl.when(here_ref[0] == here)
            def _(here=here):
                for pieces, whole in zip(parts, wholes):
                    for flip, piece in enumerate(pieces):
                        at = (here ^ flip) * some
                        whole[at : at + some, :] = piece[:some, :]

        for total in totals:
            total[...] = jnp.zeros(total.shape, F32)

    for out_ref, total, whole in zip(paired, totals, wholes):
        coupled = jnp.dot(pair_ref[...], whole[...], preferred_element_type=F32)
        own = whole[pl.ds(pl.multiple_of(step * tile, SUB), tile), :]
        own = own.astype(F32)
        total[...] += jnp.sum(own, axis=0, keepdims=True) / comps
        out_ref[...] = (own * coupled).astype(BF16)


def pair_up(here, groups, pair, tile=432):
    comps = pair.shape[0]
    sizes = [len(group) for group in groups]
    cells = [group[0].shape[1] for group in groups]
    flat = sum(groups, [])
    specs = [
        pl.BlockSpec(part.shape, lambda i: (0, 0), pipeline_mode=pl.Buffered(1)) for part in flat
    ]
    out = pl.pallas_call(
        functools.partial(pair_body, tile, sizes),
        grid=(comps // tile,),
        out_shape=[jax.ShapeDtypeStruct((comps, n), BF16) for n in cells]
        + [jax.ShapeDtypeStruct((1, n), F32) for n in cells],
        in_specs=[SMEM] + specs + [pl.BlockSpec((tile, comps), lambda i: (i, 0))],
        out_specs=[pl.BlockSpec((tile, n), lambda i: (i, 0)) for n in cells]
        + [pl.BlockSpec((1, n), lambda i: (0, 0)) for n in cells],
        scratch_shapes=[pltpu.VMEM((comps, n), BF16) for n in cells],
        compiler_params=params(20),
        cost_estimate=pl.CostEstimate(
            flops=comps * comps * sum(cells) // 4,
            bytes_accessed=comps * comps // 4,
            transcendentals=0,
        ),
    )(here, *flat, pair)
    return list(out[: len(groups)]), list(out[len(groups) :])


def apply_ranks(bounds_ref, at, which, paired, kernels, out, wide=256):
    cells = out.shape[1]
    for rank, kernel in which:
        begin, end = bounds_ref[at + rank], bounds_ref[at + rank + 1]
        for column in range(0, cells, wide):
            here = slice(column, column + wide)

            @pl.when((begin < column + wide) & (end > column))
            def _(here=here, column=column, kernel=kernel, begin=begin, end=end):
                term = jnp.dot(kernels[kernel][...], paired[:, here], preferred_element_type=F32)
                number = column + lax.broadcasted_iota(jnp.int32, term.shape, 1)
                mine = (number >= begin) & (number < end)
                out[:, here] = jnp.where(mine, term, out[:, here].astype(F32)).astype(BF16)


def product_cost(kernels, paired):
    flops = len(kernels) * kernels[0].size * sum(p.shape[1] for p in paired)
    moved = 2 * (len(kernels) * kernels[0].size + sum(p.size for p in paired))
    return pl.CostEstimate(flops=flops // 8, bytes_accessed=moved // 8, transcendentals=0)


def transfer_body(uses, strides, kept, bounds_ref, *refs):
    count, chunks = 1 + max(k for use in uses for _, k in use), len(uses)
    kernels, paired, held, outs, (mark,) = split(refs, count, chunks, len(kept), chunks, 1)
    mark[...] = jnp.zeros(mark.shape, F32)
    for chunk, out_ref in enumerate(outs):
        if chunk in kept:
            out_ref[...] = held[kept.index(chunk)][...]
        else:
            out_ref[...] = jnp.zeros(out_ref.shape, BF16)
        apply_ranks(bounds_ref, strides[chunk], uses[chunk], paired[chunk], kernels, out_ref)


def transfer(kernels, uses, strides, bounds, paired, held):
    kept = [i for i, value in enumerate(held) if value is not None]
    operands = [*kernels, *paired, *(held[i] for i in kept)]
    shapes = [jax.ShapeDtypeStruct((kernels[0].shape[0], p.shape[1]), BF16) for p in paired]
    shapes.append(jax.ShapeDtypeStruct((8, 128), F32))
    *held, mark = pl.pallas_call(
        functools.partial(transfer_body, uses, strides, kept),
        out_shape=shapes,
        in_specs=[SMEM] + [VMEM] * len(operands),
        out_specs=[VMEM] * len(shapes),
        compiler_params=params(8),
        cost_estimate=product_cost(kernels, paired),
    )(bounds, *operands)
    return held, mark


def transfer_all(kernels, first, strides, bounds, paired, held, most=6):
    mark = None
    for at in range(0, len(kernels), most):
        some = kernels[at : at + most]
        use = [(first + at + k, k) for k in range(len(some))]
        held, mark = transfer(some, [use] * len(paired), strides, bounds, paired, held)
    return held, mark


def wind_body(groups, ice_ref, speed_ref, angle_ref, *refs):
    places, outs = split(refs, len(groups), len(groups))
    maps = [speed_ref[...].astype(F32), angle_ref[...].astype(F32), ice_ref[...].astype(F32)]
    for rows, place, out_ref in zip(groups, places, outs):
        given = [cells_of(values, rows) for values in maps]
        given = jnp.concatenate(given + [jnp.zeros_like(given[0])] * 5, axis=0)
        given = put_in_order(given.astype(BF16), moves(place[...]))
        speed, angle, frozen = 0.3 * given[0:1], given[1:2], given[2:3]
        rest = [jnp.zeros_like(frozen)] * 5
        rows_out = [speed * jnp.cos(angle), speed * jnp.sin(angle), frozen] + rest
        out_ref[...] = jnp.concatenate(rows_out, axis=0)


def wind(groups, maps, places):
    return pl.pallas_call(
        functools.partial(wind_body, groups),
        out_shape=[jax.ShapeDtypeStruct((8, place.shape[1]), F32) for place in places],
        in_specs=[VMEM] * (len(maps) + len(places)),
        out_specs=[VMEM] * len(places),
        compiler_params=params(12),
        cost_estimate=pl.CostEstimate(flops=0, bytes_accessed=0, transcendentals=0),
    )(*maps, *places)


def finish_body(
    count, first, groups, strides, bounds_ref, coef_ref, *refs
):
    chunks = len(groups)
    kernels, places, winds, totals, paired, held, parts = split(
        refs, count, chunks, chunks, chunks, chunks, chunks, chunks
    )
    out_ref, *works = refs[len(refs) - 1 - chunks :]
    comps, width = out_ref.shape[1:]
    cosine, sine = coef_ref[:, 4:5], coef_ref[:, 5:6]
    for chunk, rows in enumerate(groups):
        work = works[chunk]
        work[...] = held[chunk][...]
        which = [(first + k, k) for k in range(count)]
        apply_ranks(bounds_ref, strides[chunk], which, paired[chunk], kernels, work)
        matrix = moves(places[chunk][...])
        along, across, frozen = (winds[chunk][i : i + 1, :] for i in range(3))
        total = totals[chunk][...]
        shrink = 1.0 / (1.0 + total)
        base = 1.0 - 0.5 * total * shrink
        energy = parts[chunk][:comps, :].astype(F32)
        forcing = jnp.maximum(cosine * along + sine * across, 0.0)
        result = energy * (base + forcing) + (0.2 * shrink) * work[...].astype(F32)
        result = jnp.where(frozen > 0.5, energy, result).astype(BF16)
        result = jnp.dot(result, matrix, preferred_element_type=F32).astype(BF16)
        for k, row in enumerate(rows):
            out_ref[row] = result[:, k * width : (k + 1) * width]


def finish(
    kernels, first, groups, width, strides, bounds, coef, places, winds, totals, paired, held, parts, marks
):
    comps = kernels[0].shape[0]
    rows = sum(place.shape[1] for place in places) // width
    operands = [coef, *kernels, *places, *winds, *totals, *paired, *held, *parts]
    return pl.pallas_call(
        functools.partial(finish_body, len(kernels), first, groups, strides),
        out_shape=jax.ShapeDtypeStruct((rows, comps, width), BF16),
        in_specs=[SMEM] + [VMEM] * len(operands) + [ANY] * len(marks),
        out_specs=VMEM,
        scratch_shapes=[pltpu.VMEM(value.shape, BF16) for value in held],
        compiler_params=params(20),
        cost_estimate=product_cost(kernels, paired),
    )(bounds, *operands, *marks)


def next_plane(value):
    return lax.ppermute(value, "plane", [(i, (i + 1) % PLANES) for i in range(PLANES)])


def boundaries(top, bottom):
    places = lax.axis_size("place")
    geo, count = ("plane", "place"), PLANES * places
    if places != 2:
        return (
            lax.ppermute(bottom, geo, [(i, i + 1) for i in range(count - 1)]),
            lax.ppermute(top, geo, [(i + 1, i) for i in range(count - 1)]),
        )
    first = lax.axis_index("place") == 0
    inside = lax.ppermute(jnp.where(first, bottom, top), "place", [(0, 1), (1, 0)])
    pairs = [(i, i + 1) for i in range(1, count - 1, 2)]
    outside = lax.ppermute(jnp.where(first, top, bottom), geo, pairs + [(j, i) for i, j in pairs])
    return inside, outside


def before_and_after(inside, outside):
    if lax.axis_size("place") != 2:
        return inside, outside
    first = lax.axis_index("place") == 0
    return jnp.where(first, outside, inside), jnp.where(first, inside, outside)


def with_partners(kernel):
    count = lax.axis_size("place")
    found = [kernel]
    for shift in range(1, count):
        pairs = [(i, (i + shift) % count) for i in range(count)]
        found.append(lax.ppermute(kernel, "place", pairs))
    return found


def ranks_of(owner_map):
    count = lax.axis_size("place")
    plane, place = lax.axis_index("plane"), lax.axis_index("place")
    steps = lax.rem(plane + PLANES - owner_map // count, PLANES)
    shift = lax.rem(place + count - lax.rem(owner_map, count), count)
    return steps * count + shift


def send_spec(value, flip):
    return lax.ppermute(value, "spec", [(i, i ^ flip) for i in range(4)])


def per_device(
    spectrum,
    sea_map,
    depth_factor,
    wind_speed,
    wind_dir,
    ice_mask,
    owner_map,
    pair_kernel,
    transfer_kernel,
):
    comps, rows, width = spectrum.shape
    here = lax.axis_index("spec")

    own_rows = lax.dynamic_slice_in_dim(transfer_kernel[0], here * comps, comps, axis=0)
    one_back = next_plane(own_rows)
    sea = sea_map.astype(F32)
    top = spectrum[:, 0] * sea_map[0].astype(BF16)
    bottom = spectrum[:, rows - 1] * sea_map[rows - 1].astype(BF16)
    halos = boundaries(top, bottom)
    x = spectrum.transpose(1, 0, 2)

    component = here * comps + jnp.arange(comps, dtype=jnp.int32)
    frequency = (component // NDIR).astype(F32)
    heading = 2.0 * math.pi * ((component % NDIR).astype(F32) + 0.5) / NDIR
    cosine, sine = jnp.cos(heading), jnp.sin(heading)
    gain = jnp.float32(1.1) ** (-0.5 * frequency)
    coef = jnp.stack(
        [
            0.7 * gain * jnp.abs(cosine),
            0.7 * gain * jnp.abs(sine),
            (cosine > 0).astype(F32),
            (sine > 0).astype(F32),
            cosine,
            sine,
        ],
        axis=1,
    )

    here_ref = jnp.reshape(here, (1,)).astype(jnp.int32)
    wide = 3 * rows // 8
    one, two = 1 + wide, 1 + 2 * wide
    groups = [list(range(1, one)), list(range(one, two)), [0] + list(range(two, rows))]

    def meet(part):
        return [send_spec(part, 1), send_spec(part, 2)]

    count = lax.axis_size("place")
    owners = PLANES * count
    rank_map = ranks_of(owner_map)
    kinds = jnp.arange(owners + 1, dtype=jnp.int32)
    bounds = []
    for group in groups:
        ranks = jnp.concatenate([rank_map[row] for row in group])
        bounds.append(jnp.sum((ranks[None, :] < kinds[:, None]).astype(jnp.int32), axis=1))
    bounds = jnp.concatenate(bounds)
    strides = [i * (owners + 1) for i in range(len(groups))]

    def move_rows(group, west, east):
        return propagate(
            group, owners, x, west, east, sea, depth_factor, coef, rank_map
        )

    none = jnp.zeros_like(top)
    parts, places = zip(*(move_rows(group, none, none) for group in groups[:2]))
    parts, places = list(parts), list(places)
    near = [meet(parts[0])]
    one_back, halos, near[0], sent, own_now = lax.optimization_barrier(
        (one_back, halos, near[0], parts[1], own_rows)
    )

    def pair_group(i, far):
        (more,), (total,) = pair_up(here_ref, [[parts[i], *near[i], far]], pair_kernel)
        paired.append(more)
        totals.append(total)

    paired, totals = [], []
    two_back = next_plane(one_back)
    crossed = send_spec(near[0][1], 1)
    other = send_spec(sent, 2)
    part, place = move_rows(groups[2], *before_and_after(*halos))
    crossed, sent, place = lax.optimization_barrier((crossed, sent, place))
    near.append([send_spec(sent, 1), other])
    parts.append(part)
    places.append(place)
    second = send_spec(part, 2)
    found = with_partners(own_now) + with_partners(one_back)
    marks = [value[:8, :128] for value in (found[1], found[count + 1])]
    pair_group(0, crossed)
    winds = wind(groups, [ice_mask, wind_speed, wind_dir], places)
    two_back, near[1], second, sent, totals, winds, marks = lax.optimization_barrier(
        (two_back, near[1], second, part, totals, winds, marks)
    )

    three_back = next_plane(two_back)
    later = with_partners(two_back)
    crossed = send_spec(near[1][0], 2)
    near.append([send_spec(sent, 1), second])
    last_cross = send_spec(second, 1)
    some = found + later
    held, mark = transfer_all(some, 0, strides[:1], bounds, paired, [None])
    crossed, mark = lax.optimization_barrier((crossed, mark))
    marks.append(mark)
    pair_group(1, crossed)
    more, mark = transfer_all(some, 0, strides[1:2], bounds, paired[1:2], [None])
    held += more
    last_cross, mark = lax.optimization_barrier((last_cross, mark))
    marks.append(mark)
    pair_group(2, last_cross)
    three_back, totals[2] = lax.optimization_barrier((three_back, totals[2]))
    last = with_partners(three_back)
    more, mark = transfer_all(some, 0, strides[2:], bounds, paired[2:], [None])
    held += more
    marks.append(mark)
    if last[:-2]:
        held, _ = transfer_all(last[:-2], 3 * count, strides, bounds, paired, held)
    last = last[-2:]
    out = finish(
        last,
        owners - len(last),
        groups,
        width,
        strides,
        bounds,
        coef,
        places,
        winds,
        totals,
        paired,
        held,
        parts,
        marks,
    )
    return out.transpose(1, 0, 2)


def solution(mesh):
    spec, geo = mesh.shape["spec"], mesh.shape["geo"]
    split = Mesh(
        mesh.devices.reshape(spec, PLANES, geo // PLANES), ("spec", "plane", "place")
    )
    tiles = ("plane", "place")
    placed = (
        P("spec", tiles, None),
        P(tiles, None),
        P(tiles, None),
        P(tiles, None),
        P(tiles, None),
        P(tiles, None),
        P(tiles, None),
        P(),
        P(tiles, None, None),
    )
    return jax.shard_map(
        per_device, mesh=split, in_specs=placed, out_specs=P("spec", tiles, None), check_vma=False
    )
```
